256 devices in a mesh: rep: 4 (over y_lo, core), exp: 64 (over x, y_hi, z).
Axes of the slice: x: 4, y: 4 (y_hi: 2, y_lo: 2; y = y_hi * 2 + y_lo), z: 8, core: 2. Of those that a mesh axis runs over, the one named last changes fastest.
Arguments:
- attn_out: bfloat16 [32768, 2048], P(('rep', 'exp')), may hold values from -24 to 24
- resid: bfloat16 [32768, 1024], P(('rep', 'exp')), may hold values from -6 to 6
- out_grad: bfloat16 [32768, 1024], P(('rep', 'exp')), may hold values from -6 to 6
- gain: float32 [1024], replicated, may hold values from 0.5 to 1.5
- expert_ids: int32 [32768, 8], P(('rep', 'exp')), may hold values from 0 to 63, all different within a row; in each aligned block of 128 rows (0 to 127, 128 to 255, ...) at most 18 rows name the same one
- gate_vals: float32 [32768, 8], P(('rep', 'exp')), may hold values from 0.03 to 0.5
- w_gate: bfloat16 [64, 1024, 512], P('exp'), may hold values from -0.1875 to 0.1875
- w_up: bfloat16 [64, 1024, 512], P('exp'), may hold values from -0.1875 to 0.1875
- w_down: bfloat16 [64, 512, 1024], P('exp'), may hold values from -0.25 to 0.25
Outputs:
- d_resid: bfloat16 [32768, 1024], P(('rep', 'exp'))
- projection_grad: float32 [2048, 1024], P(('rep', 'exp'))
- gate_grad: float32 [64, 1024, 512], P('exp', None, 'rep')
- up_grad: float32 [64, 1024, 512], P('exp', None, 'rep')
- down_grad: float32 [64, 512, 1024], P('exp', None, 'rep')
The draws below stay inside these ranges and needn't reach their ends.
Inputs may be any that keep to these rules, and one draw needn't show every extreme that they name: `expert_ids`: each row names 8 different experts. Among the rows of one device no expert is named more than 18 times, a bound that some block reaches.
All inputs are finite; a program needn't handle non-finite values.
Results may differ from the reference program's by a relative error of at most 0.0095.
Values may be sent and summed in bfloat16 or wider, within the bound.
No kernel may reach another device: no remote copies, remote signals or barrier semaphores. Data moves between devices by JAX's collectives and lax.ppermute only.
A program may use at most 128 MiB of HBM per device.

```python
import math
import jax
import jax.numpy as jnp
import numpy as np
from jax import lax

D = 1024
FF = 512
ATTN = 2048
TOP = 8
TOK_DEV = 128
EXPERTS = 64
CAP = 18
TOKENS = 32768
N_REP = 4
N_EXP = 64


def spiked(result, stream_key, source, target, blocks, factor):
    owner, partner = [(jnp.arange(result.shape[dim]) // (result.shape[dim] // blocks)).reshape([-1 if axis == dim else 1 for axis in range(result.ndim)]) for dim in (source, target)]
    chosen = jax.random.permutation(stream_key, blocks)[partner]
    strong = (owner == chosen) | (owner == (partner + blocks // 2) % blocks)
    return jnp.where(strong, factor * result, result)


def block_scale(key, shape, pieces, smallest, largest):
    level = 1.0
    for dim, parts in pieces:
        heights = jax.random.uniform(jax.random.fold_in(jax.random.fold_in(key, 6), dim), (parts,), jnp.float32, smallest / len(pieces), largest / len(pieces))
        level = level * jnp.repeat(jnp.exp(heights), shape[dim] // parts).reshape((-1,) + (1,) * (len(shape) - 1 - dim))
    return level


def assign_block(rng, own, number, rows, number_of, top, most, slope):
    sequence = jax.random.permutation(rng, number_of)
    packed, ordinary = portions_of(number_of, rows * top, most, slope, True), portions_of(number_of, rows * top, most, slope, False)
    places = jnp.arange(number_of)

    def named(sizes, turn):
        used = int((sizes > 0).sum())
        fixed = max(1, used // 4)
        passed = fixed + (places - fixed + turn * (used - fixed)) % max(1, number_of - fixed)
        return jnp.zeros((number_of,), jnp.int32).at[sequence[jnp.where(places < fixed, places, passed)]].set(jnp.asarray(sizes, jnp.int32))

    sizes = jnp.where(number % 4 == 0, named(packed, number // 4), named(ordinary, number - number // 4 - 1))
    mixed = jax.random.permutation(jax.random.fold_in(own, 3), number_of)
    source_of, taker = mixed[0:number_of // 2 * 2:2], mixed[1:number_of // 2 * 2:2]
    room = jnp.minimum(sizes[source_of] - 1, most - sizes[taker]) // 2
    room = jnp.where((source_of == sequence[0]) | (taker == sequence[0]) | (sizes[taker] == 0), 0, jnp.maximum(room, 0))
    passed = jax.random.randint(jax.random.fold_in(own, 4), (number_of // 2,), 0, 1 << 20) % (room + 1)
    sizes = sizes.at[source_of].add(-passed).at[taker].add(passed)
    labels = jnp.searchsorted(jnp.cumsum(sizes), jnp.arange(rows * top), side="right").astype(jnp.int32)
    grid = labels.reshape(top, rows).T
    grid = grid[jax.random.permutation(jax.random.fold_in(own, 1), rows)]
    turn = jax.random.randint(jax.random.fold_in(own, 2), (rows, 1), 0, top)
    return jnp.take_along_axis(grid, (jnp.arange(top)[None, :] + turn) % top, axis=1)


def portions_of(amount, total, limit, skew, full):
    weights = [(1 << 20) // math.isqrt(standing ** skew) + 1 for standing in range(1, amount + 1)]
    largest = limit if full else min(limit, max(-(-total // amount), total * weights[0] // sum(weights)))
    least = 1 if total - largest >= amount - 1 else 0
    given, spare = [largest] + [least] * (amount - 1), total - largest - least * (amount - 1)
    while spare > 0:
        free = [i for i in range(1, amount) if given[i] < largest] or [i for i in range(1, amount) if given[i] < limit]
        mass, left = sum([weights[i] for i in free]), spare
        for i in free:
            more = min(limit - given[i], max(1, left * weights[i] // mass), spare)
            given[i] = given[i] + more
            spare = spare - more
    return np.array(given)


def scatter_about(own_key, extent, deviation, limit, split=(), kind=jnp.bfloat16):
    result = deviation * jax.random.normal(own_key, extent, jnp.float32)
    if split:
        result = result * block_scale(own_key, extent, split, -0.22, 0.18)
    return jnp.clip(result, -limit, limit).astype(kind)


def bell_draw_with(rng, extent, scale, bound, shards, heavy, held_as=jnp.bfloat16):
    result = scale * jax.random.normal(rng, extent, jnp.float32)
    if shards:
        result = result * block_scale(rng, extent, shards, -0.22, 0.18)
    return jnp.clip(spiked(result, jax.random.fold_in(rng, 3), *heavy), -bound, bound).astype(held_as)


def setup_inputs(seed: int = 0) -> dict:
    arg_keys = jax.random.split(jax.random.key(seed), 10)
    attn_out = bell_draw_with(arg_keys[0], (TOKENS, ATTN), 1.0, 24.0, ((0, 256),), (0, 1, 256, 6.0))
    resid = scatter_about(arg_keys[1], (TOKENS, D), 1.0, 6.0, ((0, 256),))
    out_grad = scatter_about(arg_keys[2], (TOKENS, D), 1.0, 6.0, ((0, 256),))
    gain = jnp.clip(1.0 + 0.1 * jax.random.normal(arg_keys[3], (D,), jnp.float32), 0.5, 1.5)
    expert_ids_keys = jax.random.split(jax.random.fold_in(arg_keys[4], 1), TOKENS // TOK_DEV)
    expert_ids_turns = jax.random.permutation(jax.random.fold_in(arg_keys[4], 3), TOKENS // TOK_DEV)
    expert_ids = jax.vmap(lambda own, number: assign_block(jax.random.fold_in(arg_keys[4], 2), own, number, TOK_DEV, EXPERTS, TOP, CAP, 2))(expert_ids_keys, expert_ids_turns).reshape((TOKENS, TOP))
    gate_vals = jnp.clip(jnp.exp(math.log(0.5) - 2.8134107 * jax.random.uniform(arg_keys[5], (TOKENS, TOP), jnp.float32) ** block_scale(arg_keys[5], (TOKENS, TOP), ((0, 256),), -0.2, 0.2)), 0.03, 0.5)
    w_gate = scatter_about(arg_keys[6], (EXPERTS, D, FF), D ** -0.5, 0.1875, ((0, 64),))
    w_up = scatter_about(arg_keys[7], (EXPERTS, D, FF), D ** -0.5, 0.1875, ((0, 64),))
    w_down = scatter_about(arg_keys[8], (EXPERTS, FF, D), FF ** -0.5, 0.25, ((0, 64),))
    return dict(attn_out=attn_out, resid=resid, out_grad=out_grad, gain=gain, expert_ids=expert_ids, gate_vals=gate_vals, w_gate=w_gate, w_up=w_up, w_down=w_down)


epsilon = 1e-06

def slot_numbers(flat_ids, experts):
    onehot = (flat_ids[:, None] == jnp.arange(experts, dtype=jnp.int32)[None, :]).astype(jnp.int32)
    before = jnp.cumsum(onehot, axis=0) - onehot
    return lax.optimization_barrier(jnp.sum(before * onehot, axis=1)).astype(jnp.int32)

def silu_slope(pre):
    sigma = jax.nn.sigmoid(pre)
    return sigma * (1.0 + pre * (1.0 - sigma))

def expert_backward(rows_in, rows_grad, gate_matrix, up_matrix, down_matrix):
    pre_gate = jnp.dot(rows_in, gate_matrix, preferred_element_type=jnp.float32)
    pre_up = jnp.dot(rows_in, up_matrix, preferred_element_type=jnp.float32)
    active = jax.nn.silu(pre_gate)
    hidden = (active * pre_up).astype(jnp.bfloat16)
    d_hidden = jnp.dot(rows_grad, down_matrix.T, preferred_element_type=jnp.float32)
    down_part = jnp.dot(hidden.T, rows_grad, preferred_element_type=jnp.float32)
    d_gate = (d_hidden * pre_up * silu_slope(pre_gate)).astype(jnp.bfloat16)
    d_up = (d_hidden * active).astype(jnp.bfloat16)
    gate_part = jnp.dot(rows_in.T, d_gate, preferred_element_type=jnp.float32)
    up_part = jnp.dot(rows_in.T, d_up, preferred_element_type=jnp.float32)
    back = jnp.dot(d_gate, gate_matrix.T, preferred_element_type=jnp.float32)
    back = back + jnp.dot(d_up, up_matrix.T, preferred_element_type=jnp.float32)
    return (gate_part, up_part, down_part, back.astype(jnp.bfloat16))

def reference(attn_out, resid, out_grad, gain, expert_ids, gate_vals, w_gate, w_up, w_down):
    devices = N_REP * N_EXP
    per_device = TOK_DEV * TOP
    resid_f = resid.astype(jnp.float32)
    inv_rms = lax.rsqrt(lax.optimization_barrier(jnp.mean(resid_f * resid_f, axis=1, keepdims=True)) + epsilon)
    normed = resid_f * inv_rms
    gain_f = gain.astype(jnp.float32)[None, :]
    moe_in = (normed * gain_f).astype(jnp.bfloat16)
    device_ids = expert_ids.reshape(devices, per_device)
    slots = jax.vmap(lambda row_ids: slot_numbers(row_ids, EXPERTS))(device_ids)
    device_of = jnp.arange(devices, dtype=jnp.int32)[:, None]
    position = (device_of * CAP + slots).reshape(-1).astype(jnp.int32)
    table = jnp.full((EXPERTS, devices * CAP), -1, jnp.int32)
    table = table.at[expert_ids.reshape(-1), position].set(jnp.arange(TOKENS * TOP, dtype=jnp.int32))
    gate_flat = gate_vals.reshape(-1)

    def one_expert(total, inputs):
        index, gate_matrix, up_matrix, down_matrix = inputs
        valid = (index >= 0)[:, None]
        safe = jnp.maximum(index, 0).astype(jnp.int32)
        token = (safe // TOP).astype(jnp.int32)
        rows_in = jnp.where(valid, moe_in[token], jnp.zeros((), jnp.bfloat16))
        scaled = out_grad[token].astype(jnp.float32) * gate_flat[safe][:, None]
        rows_grad = jnp.where(valid, scaled, jnp.zeros((), jnp.float32)).astype(jnp.bfloat16)
        gate_part, up_part, down_part, back = expert_backward(rows_in, rows_grad, gate_matrix, up_matrix, down_matrix)
        added = jnp.where(valid, back.astype(jnp.float32), jnp.zeros((), jnp.float32))
        total = total.at[token].add(added)
        return (total, (gate_part, up_part, down_part))
    start = jnp.zeros((TOKENS, D), jnp.float32)
    d_moe, grads = lax.scan(one_expert, start, (table, w_gate, w_up, w_down))
    gate_grad, up_grad, down_grad = grads
    d_norm = d_moe * gain_f
    inner = lax.optimization_barrier(jnp.mean(d_norm * normed, axis=1, keepdims=True))
    d_resid = (out_grad.astype(jnp.float32) + inv_rms * (d_norm - normed * inner)).astype(jnp.bfloat16)
    projection_grad = jnp.dot(attn_out.T, d_resid, preferred_element_type=jnp.float32)
    return (d_resid, projection_grad, gate_grad, up_grad, down_grad)
```

```python
import jax
import jax.numpy as jnp
from jax import lax
from jax.sharding import Mesh, PartitionSpec as P

epsilon = 1e-06
AXES = ("ylo", "core", "x", "yhi", "z")
RING = 8
DELTAS = (0, -1, 1, -2, 2, -3, 3, 4)
bf16 = jnp.bfloat16
f32 = jnp.float32


def silu_slope(pre):
    sigma = jax.nn.sigmoid(pre)
    return sigma * (1.0 + pre * (1.0 - sigma))


def contract_rows(left, right):
    return lax.dot_general(left, right, (((0,), (0,)), ((), ())), preferred_element_type=f32)


def contract_last(left, right):
    return lax.dot_general(left, right, (((1,), (1,)), ((), ())), preferred_element_type=f32)


def shift_z(block, step):
    return lax.ppermute(block, "z", [(i, (i + step) % RING) for i in range(RING)])


def ring_gather(block):
    half = block.shape[1] // 2
    right, left = [block], [block]
    for _ in range(3):
        right.append(shift_z(right[-1], 1))
        left.append(shift_z(left[-1], -1))
    far_right = shift_z(right[3][:, :half], 1)
    far_left = shift_z(left[3][:, half:], -1)
    far = jnp.concatenate([far_right, far_left], axis=1)
    return [block, right[1], left[1], right[2], left[2], right[3], left[3], far]


def ring_scatter(blocks):
    half = blocks[4].shape[1] // 2
    far = blocks[4].astype(bf16)
    got = shift_z(far[:, :half], 1).astype(f32)
    right = jnp.concatenate([blocks[3][:, :half] + got, blocks[3][:, half:]], axis=1)
    got = shift_z(far[:, half:], -1).astype(f32)
    left = jnp.concatenate([blocks[-3][:, :half], blocks[-3][:, half:] + got], axis=1)
    for d in (2, 1, 0):
        got_right = shift_z(right.astype(bf16), 1).astype(f32)
        got_left = shift_z(left.astype(bf16), -1).astype(f32)
        if d:
            right = blocks[d] + got_right
            left = blocks[-d] + got_left
    return blocks[0] + got_right + got_left


def y_peer(step):
    pairs = []
    for y in range(4):
        to = (y + step) % 4
        pairs.append(((y % 2) * 2 + y // 2, (to % 2) * 2 + to // 2))
    return pairs


def swap(block, axis):
    return lax.ppermute(block, axis, [(0, 1), (1, 0)])


def body(attn_out, resid, out_grad, gain, expert_ids, gate_vals, w_gate, w_up, w_down):
    tokens, top = expert_ids.shape
    feature = resid.shape[1]
    experts = 64
    capacity = 18
    z = lax.axis_index("z")
    core = lax.axis_index("core")
    ylo = lax.axis_index("ylo")
    yhi = lax.axis_index("yhi")
    w_gate, w_up, w_down = w_gate[0], w_up[0], w_down[0]

    all_grad = lax.all_gather(out_grad, "z", axis=0, tiled=True)

    resid_f = resid.astype(f32)
    inv_rms = lax.rsqrt(jnp.mean(resid_f * resid_f, axis=1, keepdims=True) + epsilon)
    normed = resid_f * inv_rms
    gain_f = gain[None, :]
    moe_in = (normed * gain_f).astype(bf16)
    gathered = ring_gather(moe_in)

    chosen = expert_ids.T[None, :, :] == jnp.arange(experts, dtype=jnp.int32)[:, None, None]
    dense = jnp.sum(jnp.where(chosen, gate_vals.T[None, :, :], 0.0), axis=1)
    dense = dense.reshape(8, RING, tokens).transpose(1, 0, 2)
    gates = lax.all_to_all(dense, "z", split_axis=0, concat_axis=0, tiled=True)
    named = gates > 0
    before = jnp.triu(jnp.ones((tokens, tokens), bf16), 1)
    slot = lax.dot_general(
        named.astype(bf16), before, (((2,), (0,)), ((), ())), preferred_element_type=f32
    ).astype(jnp.int32)
    base = (jnp.arange(RING, dtype=jnp.int32) * capacity)[:, None, None]
    target = jnp.where(named, slot + base, -1)
    order = (z + jnp.array(DELTAS, jnp.int32)) % RING
    rows = RING * capacity
    target_rel = target[order].transpose(1, 0, 2).reshape(8, 1, RING * tokens)
    target_abs = target.transpose(1, 0, 2).reshape(8, 1, RING * tokens)
    row_ids = jnp.arange(rows, dtype=jnp.int32)[None, :, None]
    pick_rel = (row_ids == target_rel).astype(bf16)
    hit_abs = row_ids == target_abs
    gate_rows = jnp.sum(
        jnp.where(hit_abs, gates.transpose(1, 0, 2).reshape(8, 1, RING * tokens), 0.0),
        axis=2, keepdims=True,
    )

    send_in = lax.dot_general(
        pick_rel, jnp.concatenate(gathered, axis=0), (((2,), (0,)), ((), ())), preferred_element_type=bf16
    )
    got_in = lax.all_to_all(send_in, ("x", "yhi"), split_axis=0, concat_axis=0, tiled=True)
    send_grad = lax.dot_general(
        hit_abs.astype(bf16), all_grad, (((2,), (0,)), ((), ())), preferred_element_type=f32
    )
    send_grad = (send_grad * gate_rows).astype(bf16)
    got_grad = lax.all_to_all(send_grad, ("x", "yhi"), split_axis=0, concat_axis=0, tiled=True)

    rows_in = got_in.reshape(8 * rows, feature)
    rows_grad = got_grad.reshape(8 * rows, feature)
    pre_gate = jnp.dot(rows_in, w_gate, preferred_element_type=f32)
    pre_up = jnp.dot(rows_in, w_up, preferred_element_type=f32)
    active = jax.nn.silu(pre_gate)
    hidden = (active * pre_up).astype(bf16)
    d_hidden = contract_last(rows_grad, w_down)
    d_gate = (d_hidden * pre_up * silu_slope(pre_gate)).astype(bf16)
    d_up = (d_hidden * active).astype(bf16)
    back = (contract_last(d_gate, w_gate) + contract_last(d_up, w_up)).astype(bf16)
    returned = lax.all_to_all(
        back.reshape(8, rows, feature), ("x", "yhi"), split_axis=0, concat_axis=0, tiled=True
    )
    gate_part = contract_rows(rows_in, d_gate)
    up_part = contract_rows(rows_in, d_up)
    down_part = contract_rows(hidden, rows_grad)

    def over_replicas(part):
        width = part.shape[1] // 4
        blocks = part.reshape(part.shape[0], 2, 2, width)
        mine = lax.dynamic_index_in_dim(blocks, core, 2, keepdims=False)
        other = lax.dynamic_index_in_dim(blocks, 1 - core, 2, keepdims=False)
        total = mine + swap(other.astype(bf16), "core").astype(f32)
        mine = lax.dynamic_index_in_dim(total, ylo, 1, keepdims=False)
        other = lax.dynamic_index_in_dim(total, 1 - ylo, 1, keepdims=False)
        return (mine + swap(other.astype(bf16), "ylo").astype(f32))[None]

    gate_out = over_replicas(gate_part)
    up_out = over_replicas(up_part)
    down_out = over_replicas(down_part)

    terms = lax.dot_general(
        pick_rel.reshape(8 * rows, RING * tokens), returned.reshape(8 * rows, feature),
        (((0,), (0,)), ((), ())), preferred_element_type=f32,
    ).reshape(RING, tokens, feature)
    d_moe = ring_scatter({d: terms[i] for i, d in enumerate(DELTAS)})
    d_norm = d_moe * gain_f
    inner = jnp.mean(d_norm * normed, axis=1, keepdims=True)
    d_resid = (out_grad.astype(f32) + inv_rms * (d_norm - normed * inner)).astype(bf16)

    attn = attn_out.reshape(tokens, 2, 2, 4, 2, 64).transpose(1, 2, 4, 0, 3, 5).reshape(8, tokens, 256)
    attn = lax.all_to_all(attn, ("ylo", "core", "yhi"), split_axis=0, concat_axis=0, tiled=True)
    attn = attn.reshape(2, 2, 2, tokens, 256)
    y = yhi * 2 + ylo
    pieces = []
    for step in (0, 1, 3, 2):
        block = d_resid if step == 0 else lax.ppermute(d_resid, ("ylo", "yhi"), y_peer(step))
        source = (y - step) % 4
        for crossed in (0, 1):
            piece = swap(block, "core") if crossed else block
            held = attn[source % 2, (core + crossed) % 2, source // 2]
            pieces.append((held, piece))
    part = contract_rows(
        jnp.concatenate([a for a, _ in pieces], axis=0), jnp.concatenate([b for _, b in pieces], axis=0)
    )
    part = part.astype(bf16).reshape(32, 8, feature)
    part = lax.all_to_all(part, ("x", "z"), split_axis=0, concat_axis=0, tiled=True)
    projection_grad = jnp.sum(part.astype(f32), axis=0)
    return (d_resid, projection_grad, gate_out, up_out, down_out)


def solution(mesh):
    whole = Mesh(mesh.devices.reshape(2, 2, 4, 2, RING), AXES)
    tok = P(AXES, None)
    exp = ("x", "yhi", "z")
    weights = P(exp, None, None)
    in_specs = (tok, tok, tok, P(), tok, tok, weights, weights, weights)
    grads = P(exp, None, ("ylo", "core"))
    out_specs = (tok, tok, grads, grads, grads)
    return jax.shard_map(body, mesh=whole, in_specs=in_specs, out_specs=out_specs, check_vma=False)
```

```python
import functools

import jax
import jax.numpy as jnp
from jax import lax
from jax.experimental import pallas as pl
from jax.experimental.pallas import tpu as pltpu
from jax.sharding import Mesh, PartitionSpec as P

epsilon = 1e-06
AXES = ("ylo", "core", "x", "yhi", "z")
RING = 8
PLANE = 8
TOP = 8
CAPACITY = 18
META = 128
NEAR = (0, -1, 1)
FAR = (-2, 2, -3, 3, 4)
bf16 = jnp.bfloat16
f32 = jnp.float32


def contract_rows(left, right):
    return lax.dot_general(left, right, (((0,), (0,)), ((), ())), preferred_element_type=f32)


def contract_last(left, right):
    return lax.dot_general(left, right, (((1,), (1,)), ((), ())), preferred_element_type=f32)


def shift_z(block, step):
    return lax.ppermute(block, "z", [(i, (i + step) % RING) for i in range(RING)])


def swap(block, axis):
    return lax.ppermute(block, axis, [(0, 1), (1, 0)])


def y_peer(step):
    pairs = []
    for y in range(4):
        to = (y + step) % 4
        pairs.append(((y % 2) * 2 + y // 2, (to % 2) * 2 + to // 2))
    return pairs


def ring_scatter(blocks):
    half = blocks[4].shape[1] // 2
    far = blocks[4].astype(bf16)
    got = shift_z(far[:, :half], 1).astype(f32)
    right = jnp.concatenate([blocks[3][:, :half] + got, blocks[3][:, half:]], axis=1)
    got = shift_z(far[:, half:], -1).astype(f32)
    left = jnp.concatenate([blocks[-3][:, :half], blocks[-3][:, half:] + got], axis=1)
    for d in (2, 1, 0):
        got_right = shift_z(right.astype(bf16), 1).astype(f32)
        got_left = shift_z(left.astype(bf16), -1).astype(f32)
        if d:
            right = blocks[d] + got_right
            left = blocks[-d] + got_left
    return blocks[0] + got_right + got_left


def enter_kernel(resid_ref, grad_ref, gain_ref, ids_ref, vals_ref, out_ref):
    tokens, feature = resid_ref.shape
    resid = resid_ref[...].astype(f32)
    inv_rms = lax.rsqrt(jnp.mean(resid * resid, axis=1, keepdims=True) + epsilon)
    out_ref[:, :feature] = (resid * inv_rms * gain_ref[...]).astype(bf16)
    out_ref[:, feature : 2 * feature] = grad_ref[...]
    vals = vals_ref[...]
    high = vals.astype(bf16).astype(f32)
    middle = (vals - high).astype(bf16).astype(f32)
    low = vals - high - middle
    rest = jnp.zeros((tokens, META - 4 * TOP), f32)
    meta = jnp.concatenate([ids_ref[...].astype(f32), high, middle, low, rest], axis=1)
    out_ref[:, 2 * feature :] = meta.astype(bf16)


def enter(resid, out_grad, gain, expert_ids, gate_vals):
    tokens, feature = resid.shape
    return pl.pallas_call(
        enter_kernel,
        out_shape=jax.ShapeDtypeStruct((tokens, 2 * feature + META), bf16),
    )(resid, out_grad, gain.reshape(1, feature), expert_ids, gate_vals)


def pick_kernel(layout, z_ref, *refs):
    pieces = sum(len(widths) for widths in layout)
    ins, out_ref, target_ref, held, gates = refs[:pieces], *refs[pieces:]
    rows, width = out_ref.shape[1:]
    half = width // 2
    tokens = ins[0].shape[0]

    @pl.when(pl.program_id(0) == 0)
    def _():
        own = lax.broadcasted_iota(jnp.int32, (PLANE, tokens), 0) * RING + z_ref[0]
        own = own.astype(f32)
        earlier = lax.broadcasted_iota(jnp.int32, (tokens, tokens), 0)
        earlier = earlier < lax.broadcasted_iota(jnp.int32, (tokens, tokens), 1)
        earlier = jnp.where(earlier, 1.0, 0.0).astype(bf16)
        at = 0
        for i, widths in enumerate(layout):
            lines = slice(i * tokens, (i + 1) * tokens)
            column = 0
            for piece in widths:
                ref = ins[at]
                data = piece
                if column + piece > width:
                    data = width - column
                    meta = ref[:, data:]
                held[lines, column : column + data] = ref[:, :data]
                column += data
                at += 1
            meta = meta.astype(f32).T
            value = meta[TOP : 2 * TOP] + meta[2 * TOP : 3 * TOP] + meta[3 * TOP : 4 * TOP]
            named = jnp.zeros((PLANE, tokens), f32)
            gate = jnp.zeros((PLANE, tokens), f32)
            for k in range(TOP):
                same = meta[k : k + 1] == own
                named = jnp.where(same, 1.0, named)
                gate = jnp.where(same, value[k : k + 1], gate)
            slot = jnp.dot(named.astype(bf16), earlier, preferred_element_type=f32)
            place = jnp.where(named > 0.5, slot + float(i * CAPACITY), -1.0)
            target_ref[:, lines] = place
            gates[:, lines] = gate

    e = pl.program_id(0)
    row_ids = lax.broadcasted_iota(jnp.int32, (rows, held.shape[0]), 0).astype(f32)
    hit = row_ids == target_ref[pl.ds(e, 1), :]
    gate = jnp.sum(jnp.where(hit, gates[pl.ds(e, 1), :], 0.0), axis=1, keepdims=True)
    onehot = jnp.where(hit, 1.0, 0.0).astype(bf16)
    picked = jnp.dot(onehot, held[:, :half], preferred_element_type=f32)
    out_ref[0, :, :half] = picked.astype(bf16)
    picked = jnp.dot(onehot, held[:, half:], preferred_element_type=f32)
    out_ref[0, :, half:] = (picked * gate).astype(bf16)


def pick_rows(z, blocks, width):
    count = len(blocks)
    tokens = blocks[0][0].shape[0]
    rows = -(-count * CAPACITY // 8) * 8
    flat = [piece for block in blocks for piece in block]
    layout = tuple(tuple(piece.shape[1] for piece in block) for block in blocks)
    whole = [pl.BlockSpec(piece.shape, lambda e, z: (0, 0)) for piece in flat]
    return pl.pallas_call(
        functools.partial(pick_kernel, layout),
        grid_spec=pltpu.PrefetchScalarGridSpec(
            num_scalar_prefetch=1,
            grid=(PLANE,),
            in_specs=whole,
            out_specs=[
                pl.BlockSpec((1, rows, width), lambda e, z: (e, 0, 0)),
                pl.BlockSpec((PLANE, count * tokens), lambda e, z: (0, 0)),
            ],
            scratch_shapes=[
                pltpu.VMEM((count * tokens, width), bf16),
                pltpu.VMEM((PLANE, count * tokens), f32),
            ],
        ),
        out_shape=[
            jax.ShapeDtypeStruct((PLANE, rows, width), bf16),
            jax.ShapeDtypeStruct((PLANE, count * tokens), f32),
        ],
        compiler_params=pltpu.CompilerParams(vmem_limit_bytes=24 << 20),
        cost_estimate=pl.CostEstimate(
            flops=2 * PLANE * rows * count * tokens * width,
            bytes_accessed=2 * width * (count * tokens + PLANE * rows),
            transcendentals=0,
        ),
    )(z.reshape(1), *flat)


def expert_kernel(got_ref, w_gate_ref, w_up_ref, w_down_ref, back_ref, slopes_ref, hidden_ref):
    feature = back_ref.shape[1]
    inner = hidden_ref.shape[1]
    rows_in, rows_grad = got_ref[:, :feature], got_ref[:, feature:]
    pre_gate = jnp.dot(rows_in, w_gate_ref[...], preferred_element_type=f32)
    pre_up = jnp.dot(rows_in, w_up_ref[...], preferred_element_type=f32)
    d_hidden = contract_last(rows_grad, w_down_ref[...])
    sigma = jax.nn.sigmoid(pre_gate)
    active = pre_gate * sigma
    hidden_ref[...] = (active * pre_up).astype(bf16)
    d_gate = (d_hidden * pre_up * (sigma * (1.0 + pre_gate * (1.0 - sigma)))).astype(bf16)
    d_up = (d_hidden * active).astype(bf16)
    for i in range(inner // 128):
        slopes_ref[:, 256 * i : 256 * i + 128] = d_gate[:, 128 * i : 128 * i + 128]
        slopes_ref[:, 256 * i + 128 : 256 * i + 256] = d_up[:, 128 * i : 128 * i + 128]
    back = contract_last(d_gate, w_gate_ref[...]) + contract_last(d_up, w_up_ref[...])
    back_ref[...] = back.astype(bf16)


def run_expert(got, w_gate, w_up, w_down, steps):
    total, width = got.shape
    feature, inner = w_gate.shape
    rows = total // steps
    return pl.pallas_call(
        expert_kernel,
        grid=(steps,),
        in_specs=[
            pl.BlockSpec((rows, width), lambda i: (i, 0)),
            pl.BlockSpec((feature, inner), lambda i: (0, 0)),
            pl.BlockSpec((feature, inner), lambda i: (0, 0)),
            pl.BlockSpec((inner, feature), lambda i: (0, 0)),
        ],
        out_specs=[
            pl.BlockSpec((rows, feature), lambda i: (i, 0)),
            pl.BlockSpec((rows, 2 * inner), lambda i: (i, 0)),
            pl.BlockSpec((rows, inner), lambda i: (i, 0)),
        ],
        out_shape=[
            jax.ShapeDtypeStruct((total, feature), bf16),
            jax.ShapeDtypeStruct((total, 2 * inner), bf16),
            jax.ShapeDtypeStruct((total, inner), bf16),
        ],
        compiler_params=pltpu.CompilerParams(vmem_limit_bytes=32 << 20),
        cost_estimate=pl.CostEstimate(
            flops=10 * total * feature * inner,
            bytes_accessed=2 * total * (width + feature + 3 * inner) + 6 * feature * inner,
            transcendentals=total * inner,
        ),
    )(got, w_gate, w_up, w_down)


def weights_kernel(core_ref, *refs):
    (x1, g1, s1, h1, x2, g2, s2, h2, other_ref, mine_ref) = refs
    feature = x1.shape[1]
    top = contract_rows(x1[...], s1[...]) + contract_rows(x2[...], s2[...])
    low = contract_rows(h1[...], g1[...]) + contract_rows(h2[...], g2[...])

    @pl.when(pl.program_id(0) < 2)
    def _():
        other_ref[0, :feature, :] = top.astype(bf16)
        other_ref[0, feature:, :] = low.astype(bf16)

    @pl.when(pl.program_id(0) >= 2)
    def _():
        mine_ref[0, :feature, :] = top
        mine_ref[0, feature:, :] = low


def weight_terms(core, near, far):
    specs, arrays, flops = [], [], 0
    for got, slopes, hidden in (near, far):
        rows, width = got.shape
        feature = width // 2
        inner = hidden.shape[1]
        share = feature // 4

        def block(s, core):
            return (s % 2) * 2 + jnp.where(s < 2, 1 - core[0], core[0])

        specs += [
            pl.BlockSpec((rows, feature), lambda s, core: (0, 0)),
            pl.BlockSpec((rows, share), lambda s, core: (0, 4 + block(s, core))),
            pl.BlockSpec((rows, share), lambda s, core: (0, block(s, core))),
            pl.BlockSpec((rows, inner), lambda s, core: (0, 0)),
        ]
        arrays += [got, got, slopes, hidden]
        flops += 2 * rows * feature * 3 * inner
    shape = (2, feature + inner, share)
    return pl.pallas_call(
        weights_kernel,
        grid_spec=pltpu.PrefetchScalarGridSpec(
            num_scalar_prefetch=1,
            grid=(4,),
            in_specs=specs,
            out_specs=[
                pl.BlockSpec((1,) + shape[1:], lambda s, core: (jnp.minimum(s, 1), 0, 0)),
                pl.BlockSpec((1,) + shape[1:], lambda s, core: (jnp.maximum(s - 2, 0), 0, 0)),
            ],
        ),
        out_shape=[jax.ShapeDtypeStruct(shape, bf16), jax.ShapeDtypeStruct(shape, f32)],
        compiler_params=pltpu.CompilerParams(vmem_limit_bytes=40 << 20),
        cost_estimate=pl.CostEstimate(flops=flops, bytes_accessed=16 << 20, transcendentals=0),
    )(core.reshape(1), *arrays)


def body(attn_out, resid, out_grad, gain, expert_ids, gate_vals, w_gate, w_up, w_down):
    tokens, feature = resid.shape
    z = lax.axis_index("z")
    core = lax.axis_index("core")
    ylo = lax.axis_index("ylo")
    yhi = lax.axis_index("yhi")
    w_gate, w_up, w_down = w_gate[0], w_up[0], w_down[0]

    mine = enter(resid, out_grad, gain, expert_ids, gate_vals)
    right, left = shift_z(mine, 1), shift_z(mine, -1)
    attn = attn_out.reshape(tokens, 2, 2, 4, 2, 64).transpose(1, 2, 4, 0, 3, 5).reshape(8, tokens, 256)
    attn = lax.all_to_all(attn, ("ylo", "core", "yhi"), split_axis=0, concat_axis=0, tiled=True)
    right, left, attn = lax.optimization_barrier((right, left, attn))
    gathered = {0: [mine], -1: [right], 1: [left]}
    for d in (2, 3):
        right, left = shift_z(right, 1), shift_z(left, -1)
        gathered[-d], gathered[d] = [right], [left]
    gathered[4] = [shift_z(right[:, :feature], 1), shift_z(left[:, feature:], -1)]

    def send(deltas):
        sent, target = pick_rows(z, [gathered[d] for d in deltas], 2 * feature)
        got = lax.all_to_all(sent, ("x", "yhi"), split_axis=0, concat_axis=0, tiled=True)
        return got.reshape(-1, 2 * feature), target

    def answer(got, steps):
        back, slopes, hidden = run_expert(got, w_gate, w_up, w_down, steps)
        back = back.reshape(PLANE, -1, feature)
        returned = lax.all_to_all(back, ("x", "yhi"), split_axis=0, concat_axis=0, tiled=True)
        return returned, (got, slopes, hidden)

    got_near, target_near = send(NEAR)
    got_far, target_far = send(FAR)
    returned_near, saved_near = answer(got_near, 2)
    returned_far, saved_far = answer(got_far, 3)
    other, own = weight_terms(core, saved_near, saved_far)
    returned_far, other, own = lax.optimization_barrier((returned_far, other, own))

    total = own + swap(other, "core").astype(f32)
    held = lax.dynamic_index_in_dim(total, ylo, 0, keepdims=False)
    other = lax.dynamic_index_in_dim(total, 1 - ylo, 0, keepdims=False)
    total = held + swap(other.astype(bf16), "ylo").astype(f32)
    half = total.shape[1] // 2
    gate_out, up_out, down_out = total[None, :feature, :half], total[None, :feature, half:], total[None, feature:]

    terms = {}
    for target, deltas, returned in ((target_near, NEAR, returned_near), (target_far, FAR, returned_far)):
        rows = returned.shape[1]
        pick = (jnp.arange(rows, dtype=jnp.int32).astype(f32)[None, :, None] == target[:, None, :]).astype(bf16)
        term = contract_rows(pick.reshape(PLANE * rows, -1), returned.reshape(PLANE * rows, feature))
        for i, d in enumerate(deltas):
            terms[d] = term[i * tokens : (i + 1) * tokens]
    d_moe = ring_scatter(terms)
    gain_f = gain[None, :]
    resid_f = resid.astype(f32)
    inv_rms = lax.rsqrt(jnp.mean(resid_f * resid_f, axis=1, keepdims=True) + epsilon)
    normed = resid_f * inv_rms
    d_norm = d_moe * gain_f
    inner = jnp.mean(d_norm * normed, axis=1, keepdims=True)
    d_resid = (out_grad.astype(f32) + inv_rms * (d_norm - normed * inner)).astype(bf16)

    attn = attn.reshape(2, 2, 2, tokens, 256)
    y = yhi * 2 + ylo
    pieces = []
    for step in (0, 1, 3, 2):
        block = d_resid if step == 0 else lax.ppermute(d_resid, ("ylo", "yhi"), y_peer(step))
        source = (y - step) % 4
        for crossed in (0, 1):
            piece = swap(block, "core") if crossed else block
            held = attn[source % 2, (core + crossed) % 2, source // 2]
            pieces.append((held, piece))
    part = contract_rows(
        jnp.concatenate([a for a, _ in pieces], axis=0), jnp.concatenate([b for _, b in pieces], axis=0)
    )
    part = part.astype(bf16).reshape(32, 8, feature)
    part = lax.all_to_all(part, ("x", "z"), split_axis=0, concat_axis=0, tiled=True)
    projection_grad = jnp.sum(part.astype(f32), axis=0)
    return (d_resid, projection_grad, gate_out, up_out, down_out)


def solution(mesh):
    whole = Mesh(mesh.devices.reshape(2, 2, 4, 2, RING), AXES)
    tok = P(AXES, None)
    exp = ("x", "yhi", "z")
    weights = P(exp, None, None)
    in_specs = (tok, tok, tok, P(), tok, tok, weights, weights, weights)
    grads = P(exp, None, ("ylo", "core"))
    out_specs = (tok, tok, grads, grads, grads)
    return jax.shard_map(body, mesh=whole, in_specs=in_specs, out_specs=out_specs, check_vma=False)
```

```python
import functools

import jax
import jax.numpy as jnp
from jax import lax
from jax.experimental import pallas as pl
from jax.experimental.pallas import tpu as pltpu
from jax.sharding import Mesh, PartitionSpec as P

epsilon = 1e-06
AXES = ("ylo", "core", "x", "yhi", "z")
RING = 8
PLANE = 8
TOP = 8
CAPACITY = 18
META = 128
NEAR = (0, -1, 1)
FAR = (-2, 2, -3, 3, 4)
bf16 = jnp.bfloat16
f32 = jnp.float32


def contract_rows(left, right):
    return lax.dot_general(left, right, (((0,), (0,)), ((), ())), preferred_element_type=f32)


def contract_last(left, right):
    return lax.dot_general(left, right, (((1,), (1,)), ((), ())), preferred_element_type=f32)


def shift_z(block, step):
    return lax.ppermute(block, "z", [(i, (i + step) % RING) for i in range(RING)])


def swap(block, axis):
    return lax.ppermute(block, axis, [(0, 1), (1, 0)])


def y_peer(step):
    pairs = []
    for y in range(4):
        to = (y + step) % 4
        pairs.append(((y % 2) * 2 + y // 2, (to % 2) * 2 + to // 2))
    return pairs


def ring_scatter(blocks):
    half = blocks[4].shape[1] // 2
    far = blocks[4].astype(bf16)
    got = shift_z(far[:, :half], 1).astype(f32)
    right = jnp.concatenate([blocks[3][:, :half] + got, blocks[3][:, half:]], axis=1)
    got = shift_z(far[:, half:], -1).astype(f32)
    left = jnp.concatenate([blocks[-3][:, :half], blocks[-3][:, half:] + got], axis=1)
    for d in (2, 1, 0):
        got_right = shift_z(right.astype(bf16), 1).astype(f32)
        got_left = shift_z(left.astype(bf16), -1).astype(f32)
        if d:
            right = blocks[d] + got_right
            left = blocks[-d] + got_left
    return blocks[0] + got_right + got_left


def enter_kernel(resid_ref, grad_ref, gain_ref, ids_ref, vals_ref, in_ref, out_ref):
    tokens, feature = resid_ref.shape
    resid = resid_ref[...].astype(f32)
    inv_rms = lax.rsqrt(jnp.mean(resid * resid, axis=1, keepdims=True) + epsilon)
    in_ref[...] = (resid * inv_rms * gain_ref[...]).astype(bf16)
    out_ref[:, :feature] = grad_ref[...]
    vals = vals_ref[...]
    high = vals.astype(bf16).astype(f32)
    middle = (vals - high).astype(bf16).astype(f32)
    low = vals - high - middle
    rest = jnp.zeros((META - 4 * TOP, tokens), f32)
    meta = jnp.concatenate([ids_ref[...].astype(f32), high, middle, low, rest], axis=0)
    out_ref[:, feature:] = meta.T.astype(bf16)


def enter(resid, out_grad, gain, expert_ids, gate_vals):
    tokens, feature = resid.shape
    return pl.pallas_call(
        enter_kernel,
        out_shape=[
            jax.ShapeDtypeStruct((tokens, feature), bf16),
            jax.ShapeDtypeStruct((tokens, feature + META), bf16),
        ],
    )(resid, out_grad, gain.reshape(1, feature), expert_ids.T, gate_vals.T)


def pick_kernel(layout, first, offset, z_ref, *refs):
    pieces = sum(len(widths) for widths in layout)
    ins, (out_ref, target_ref, held, gates) = refs[:pieces], refs[-4:]
    rows, width = out_ref.shape[1:]
    half = width // 2
    tokens = ins[0].shape[0]

    @pl.when(pl.program_id(0) == 0)
    def _():
        own = lax.broadcasted_iota(jnp.int32, (PLANE, tokens), 0) * RING + z_ref[0]
        own = own.astype(f32)
        earlier = lax.broadcasted_iota(jnp.int32, (tokens, tokens), 0)
        earlier = earlier < lax.broadcasted_iota(jnp.int32, (tokens, tokens), 1)
        earlier = jnp.where(earlier, 1.0, 0.0).astype(bf16)
        at = 0
        for i, widths in enumerate(layout):
            lines = slice(i * tokens, (i + 1) * tokens)
            column = 0
            for piece in widths:
                ref = ins[at]
                data = piece
                if column + piece > width:
                    data = width - column
                    meta = ref[:, data:]
                held[lines, column : column + data] = ref[:, :data]
                column += data
                at += 1
            meta = meta.astype(f32).T
            value = meta[TOP : 2 * TOP] + meta[2 * TOP : 3 * TOP] + meta[3 * TOP : 4 * TOP]
            named = jnp.zeros((PLANE, tokens), f32)
            gate = jnp.zeros((PLANE, tokens), f32)
            for k in range(TOP):
                same = meta[k : k + 1] == own
                named = jnp.where(same, 1.0, named)
                gate = jnp.where(same, value[k : k + 1], gate)
            slot = jnp.dot(named.astype(bf16), earlier, preferred_element_type=f32)
            place = jnp.where(named > 0.5, slot + float((first + i) * CAPACITY), -1.0)
            target_ref[:, lines] = place
            gates[:, lines] = gate

    e = pl.program_id(0)
    row_ids = (lax.broadcasted_iota(jnp.int32, (rows, held.shape[0]), 0) + offset).astype(f32)
    hit = row_ids == target_ref[pl.ds(e, 1), :]
    gate = jnp.sum(jnp.where(hit, gates[pl.ds(e, 1), :], 0.0), axis=1, keepdims=True)
    onehot = jnp.where(hit, 1.0, 0.0).astype(bf16)
    picked = jnp.dot(onehot, held[:, :half], preferred_element_type=f32)
    out_ref[0, :, :half] = picked.astype(bf16)
    picked = jnp.dot(onehot, held[:, half:], preferred_element_type=f32)
    out_ref[0, :, half:] = (picked * gate).astype(bf16)


def pick_rows(z, blocks, width, total, first=0, rows=None, into=None):
    count = len(blocks)
    tokens = blocks[0][0].shape[0]
    rows = rows or total
    at = total // rows - 1
    flat = [piece for block in blocks for piece in block]
    layout = tuple(tuple(piece.shape[1] for piece in block) for block in blocks)
    whole = [pl.BlockSpec(piece.shape, lambda e, z: (0, 0)) for piece in flat]
    return pl.pallas_call(
        functools.partial(pick_kernel, layout, first, total - rows),
        grid_spec=pltpu.PrefetchScalarGridSpec(
            num_scalar_prefetch=1,
            grid=(PLANE,),
            in_specs=whole + [pl.BlockSpec(memory_space=pl.ANY)] * (into is not None),
            out_specs=[
                pl.BlockSpec((1, rows, width), lambda e, z: (e, at, 0)),
                pl.BlockSpec((PLANE, count * tokens), lambda e, z: (0, 0)),
            ],
            scratch_shapes=[
                pltpu.VMEM((count * tokens, width), bf16),
                pltpu.VMEM((PLANE, count * tokens), f32),
            ],
        ),
        out_shape=[
            jax.ShapeDtypeStruct((PLANE, total, width), bf16),
            jax.ShapeDtypeStruct((PLANE, count * tokens), f32),
        ],
        input_output_aliases={} if into is None else {1 + len(flat): 0},
        compiler_params=pltpu.CompilerParams(vmem_limit_bytes=56 << 20),
        cost_estimate=pl.CostEstimate(
            flops=2 * PLANE * rows * count * tokens * width,
            bytes_accessed=2 * width * (count * tokens + PLANE * rows),
            transcendentals=0,
        ),
    )(z.reshape(1), *flat, *([] if into is None else [into]))


def expert_kernel(got_ref, w_gate_ref, w_up_ref, w_down_ref, back_ref, slopes_ref, hidden_ref):
    feature = back_ref.shape[1]
    inner = hidden_ref.shape[1]
    rows_in, rows_grad = got_ref[:, :feature], got_ref[:, feature:]
    pre_gate = jnp.dot(rows_in, w_gate_ref[...], preferred_element_type=f32)
    pre_up = jnp.dot(rows_in, w_up_ref[...], preferred_element_type=f32)
    d_hidden = contract_last(rows_grad, w_down_ref[...])
    sigma = jax.nn.sigmoid(pre_gate)
    active = pre_gate * sigma
    hidden_ref[...] = (active * pre_up).astype(bf16)
    d_gate = (d_hidden * pre_up * (sigma * (1.0 + pre_gate * (1.0 - sigma)))).astype(bf16)
    d_up = (d_hidden * active).astype(bf16)
    for i in range(inner // 128):
        slopes_ref[:, 256 * i : 256 * i + 128] = d_gate[:, 128 * i : 128 * i + 128]
        slopes_ref[:, 256 * i + 128 : 256 * i + 256] = d_up[:, 128 * i : 128 * i + 128]
    back = contract_last(d_gate, w_gate_ref[...]) + contract_last(d_up, w_up_ref[...])
    back_ref[...] = back.astype(bf16)


def run_expert(got, w_gate, w_up, w_down, steps):
    total, width = got.shape
    feature, inner = w_gate.shape
    rows = total // steps
    return pl.pallas_call(
        expert_kernel,
        grid=(steps,),
        in_specs=[
            pl.BlockSpec((rows, width), lambda i: (i, 0)),
            pl.BlockSpec((feature, inner), lambda i: (0, 0)),
            pl.BlockSpec((feature, inner), lambda i: (0, 0)),
            pl.BlockSpec((inner, feature), lambda i: (0, 0)),
        ],
        out_specs=[
            pl.BlockSpec((rows, feature), lambda i: (i, 0)),
            pl.BlockSpec((rows, 2 * inner), lambda i: (i, 0)),
            pl.BlockSpec((rows, inner), lambda i: (i, 0)),
        ],
        out_shape=[
            jax.ShapeDtypeStruct((total, feature), bf16),
            jax.ShapeDtypeStruct((total, 2 * inner), bf16),
            jax.ShapeDtypeStruct((total, inner), bf16),
        ],
        compiler_params=pltpu.CompilerParams(vmem_limit_bytes=56 << 20),
        cost_estimate=pl.CostEstimate(
            flops=10 * total * feature * inner,
            bytes_accessed=2 * total * (width + feature + 3 * inner) + 6 * feature * inner,
            transcendentals=total * inner,
        ),
    )(got, w_gate, w_up, w_down)


def weights_kernel(core_ref, *refs):
    (x1, g1, s1, h1, x2, g2, s2, h2, other_ref, mine_ref) = refs
    feature = x1.shape[1]
    top = contract_rows(x1[...], s1[...]) + contract_rows(x2[...], s2[...])
    low = contract_rows(h1[...], g1[...]) + contract_rows(h2[...], g2[...])

    @pl.when(pl.program_id(0) < 2)
    def _():
        other_ref[0, :feature, :] = top.astype(bf16)
        other_ref[0, feature:, :] = low.astype(bf16)

    @pl.when(pl.program_id(0) >= 2)
    def _():
        mine_ref[0, :feature, :] = top
        mine_ref[0, feature:, :] = low


def weight_terms(core, near, far):
    specs, arrays, flops = [], [], 0
    for got, slopes, hidden in (near, far):
        rows, width = got.shape
        feature = width // 2
        inner = hidden.shape[1]
        share = feature // 4

        def block(s, core):
            return (s % 2) * 2 + jnp.where(s < 2, 1 - core[0], core[0])

        specs += [
            pl.BlockSpec((rows, feature), lambda s, core: (0, 0)),
            pl.BlockSpec((rows, share), lambda s, core: (0, 4 + block(s, core))),
            pl.BlockSpec((rows, share), lambda s, core: (0, block(s, core))),
            pl.BlockSpec((rows, inner), lambda s, core: (0, 0)),
        ]
        arrays += [got, got, slopes, hidden]
        flops += 2 * rows * feature * 3 * inner
    shape = (2, feature + inner, share)
    return pl.pallas_call(
        weights_kernel,
        grid_spec=pltpu.PrefetchScalarGridSpec(
            num_scalar_prefetch=1,
            grid=(4,),
            in_specs=specs,
            out_specs=[
                pl.BlockSpec((1,) + shape[1:], lambda s, core: (jnp.minimum(s, 1), 0, 0)),
                pl.BlockSpec((1,) + shape[1:], lambda s, core: (jnp.maximum(s - 2, 0), 0, 0)),
            ],
        ),
        out_shape=[jax.ShapeDtypeStruct(shape, bf16), jax.ShapeDtypeStruct(shape, f32)],
        compiler_params=pltpu.CompilerParams(vmem_limit_bytes=56 << 20),
        cost_estimate=pl.CostEstimate(flops=flops, bytes_accessed=16 << 20, transcendentals=0),
    )(core.reshape(1), *arrays)


def body(attn_out, resid, out_grad, gain, expert_ids, gate_vals, w_gate, w_up, w_down):
    tokens, feature = resid.shape
    z = lax.axis_index("z")
    core = lax.axis_index("core")
    ylo = lax.axis_index("ylo")
    yhi = lax.axis_index("yhi")
    w_gate, w_up, w_down = w_gate[0], w_up[0], w_down[0]

    own = enter(resid, out_grad, gain, expert_ids, gate_vals)
    right, left = [shift_z(a, 1) for a in own], [shift_z(a, -1) for a in own]
    gathered = {0: own, -1: right, 1: left}
    sent_near, target_near = pick_rows(z, [gathered[d] for d in NEAR], 2 * feature, 56)
    attn = attn_out.reshape(tokens, 2, 2, 4, 2, 64).transpose(1, 2, 4, 0, 3, 5).reshape(8, tokens, 256)
    attn = lax.all_to_all(attn, ("ylo", "core", "yhi"), split_axis=0, concat_axis=0, tiled=True)
    right, left = [shift_z(a, 1) for a in right], [shift_z(a, -1) for a in left]
    sent_near, attn, right, left = lax.optimization_barrier((sent_near, attn, right, left))
    gathered[-2], gathered[2] = right, left
    right, left = [shift_z(a, 1) for a in right], [shift_z(a, -1) for a in left]
    gathered[-3], gathered[3] = right, left
    sent_far, target_far = pick_rows(z, [gathered[d] for d in FAR[:-1]], 2 * feature, 96)
    sent_far, *last = lax.optimization_barrier((sent_far, shift_z(right[0], 1), shift_z(left[1], -1)))
    last = [gathered[3], last]
    sent_far, target_last = pick_rows(z, last, 2 * feature, 96, len(FAR) - 2, 32, sent_far)
    target_far = jnp.concatenate([target_far, target_last[:, tokens:]], axis=1)

    def over_plane(rows):
        return lax.all_to_all(rows, ("x", "yhi"), split_axis=0, concat_axis=0, tiled=True)

    got_near = over_plane(sent_near).reshape(-1, 2 * feature)
    got_near, sent_far = lax.optimization_barrier((got_near, sent_far))
    got_far = over_plane(sent_far).reshape(-1, 2 * feature)
    back_near, *saved_near = run_expert(got_near, w_gate, w_up, w_down, 2)
    back_near, got_far = lax.optimization_barrier((back_near, got_far))
    returned_near = over_plane(back_near.reshape(PLANE, -1, feature))
    back_far, *saved_far = run_expert(got_far, w_gate, w_up, w_down, 3)
    returned_near, back_far = lax.optimization_barrier((returned_near, back_far))
    returned_far = over_plane(back_far.reshape(PLANE, -1, feature))
    other, own = weight_terms(core, (got_near, *saved_near), (got_far, *saved_far))
    returned_far, other, own = lax.optimization_barrier((returned_far, other, own))

    total = own + swap(other, "core").astype(f32)
    held = lax.dynamic_index_in_dim(total, ylo, 0, keepdims=False)
    other = lax.dynamic_index_in_dim(total, 1 - ylo, 0, keepdims=False)
    total = held + swap(other.astype(bf16), "ylo").astype(f32)
    half = total.shape[1] // 2
    gate_out, up_out, down_out = total[None, :feature, :half], total[None, :feature, half:], total[None, feature:]

    terms = {}
    for target, deltas, returned in ((target_near, NEAR, returned_near), (target_far, FAR, returned_far)):
        rows = returned.shape[1]
        pick = (jnp.arange(rows, dtype=jnp.int32).astype(f32)[None, :, None] == target[:, None, :]).astype(bf16)
        term = contract_rows(pick.reshape(PLANE * rows, -1), returned.reshape(PLANE * rows, feature))
        for i, d in enumerate(deltas):
            terms[d] = term[i * tokens : (i + 1) * tokens]
    d_moe = ring_scatter(terms)
    gain_f = gain[None, :]
    resid_f = resid.astype(f32)
    inv_rms = lax.rsqrt(jnp.mean(resid_f * resid_f, axis=1, keepdims=True) + epsilon)
    normed = resid_f * inv_rms
    d_norm = d_moe * gain_f
    inner = jnp.mean(d_norm * normed, axis=1, keepdims=True)
    d_resid = (out_grad.astype(f32) + inv_rms * (d_norm - normed * inner)).astype(bf16)

    attn = attn.reshape(2, 2, 2, tokens, 256)
    y = yhi * 2 + ylo
    pieces = []
    for step in (0, 1, 3, 2):
        block = d_resid if step == 0 else lax.ppermute(d_resid, ("ylo", "yhi"), y_peer(step))
        source = (y - step) % 4
        for crossed in (0, 1):
            piece = swap(block, "core") if crossed else block
            held = attn[source % 2, (core + crossed) % 2, source // 2]
            pieces.append((held, piece))
    part = contract_rows(
        jnp.concatenate([a for a, _ in pieces], axis=0), jnp.concatenate([b for _, b in pieces], axis=0)
    )
    part = part.astype(bf16).reshape(32, 8, feature)
    part = lax.all_to_all(part, ("x", "z"), split_axis=0, concat_axis=0, tiled=True)
    projection_grad = jnp.sum(part.astype(f32), axis=0)
    return (d_resid, projection_grad, gate_out, up_out, down_out)


def solution(mesh):
    whole = Mesh(mesh.devices.reshape(2, 2, 4, 2, RING), AXES)
    tok = P(AXES, None)
    exp = ("x", "yhi", "z")
    weights = P(exp, None, None)
    in_specs = (tok, tok, tok, P(), tok, tok, weights, weights, weights)
    grads = P(exp, None, ("ylo", "core"))
    out_specs = (tok, tok, grads, grads, grads)
    return jax.shard_map(body, mesh=whole, in_specs=in_specs, out_specs=out_specs, check_vma=False)
```

```python
import functools

import jax
import jax.numpy as jnp
from jax import lax
from jax.experimental import pallas as pl
from jax.experimental.pallas import tpu as pltpu
from jax.sharding import Mesh, PartitionSpec as P

epsilon = 1e-06
AXES = ("ylo", "core", "x", "yhi", "z")
RING = 8
PLANE = 8
TOP = 8
CAPACITY = 18
META = 128
NEAR = (0, -1, 1)
FAR = (-2, 2, -3, 3, 4)
bf16 = jnp.bfloat16
f32 = jnp.float32


def contract_rows(left, right):
    return lax.dot_general(left, right, (((0,), (0,)), ((), ())), preferred_element_type=f32)


def contract_last(left, right):
    return lax.dot_general(left, right, (((1,), (1,)), ((), ())), preferred_element_type=f32)


def shift_z(block, step):
    return lax.ppermute(block, "z", [(i, (i + step) % RING) for i in range(RING)])


def swap(block, axis):
    return lax.ppermute(block, axis, [(0, 1), (1, 0)])


def y_peer(step):
    pairs = []
    for y in range(4):
        to = (y + step) % 4
        pairs.append(((y % 2) * 2 + y // 2, (to % 2) * 2 + to // 2))
    return pairs


def ring_scatter(blocks, later):
    half = blocks[4].shape[1] // 2
    far = blocks[4].astype(bf16)
    got = shift_z(far[:, :half], 1).astype(f32)
    right = jnp.concatenate([blocks[3][:, :half] + got, blocks[3][:, half:]], axis=1)
    got = shift_z(far[:, half:], -1).astype(f32)
    left = jnp.concatenate([blocks[-3][:, :half], blocks[-3][:, half:] + got], axis=1)
    for d in (2, 1):
        right = blocks[d] + shift_z(right.astype(bf16), 1).astype(f32)
        left = blocks[-d] + shift_z(left.astype(bf16), -1).astype(f32)
    right, left, later = lax.optimization_barrier((right.astype(bf16), left.astype(bf16), later))
    right, left = shift_z(right, 1), shift_z(left, -1)
    return blocks[0] + right.astype(f32) + left.astype(f32), later


def enter_kernel(resid_ref, grad_ref, gain_ref, ids_ref, vals_ref, in_ref, out_ref):
    tokens, feature = resid_ref.shape
    resid = resid_ref[...].astype(f32)
    inv_rms = lax.rsqrt(jnp.mean(resid * resid, axis=1, keepdims=True) + epsilon)
    in_ref[...] = (resid * inv_rms * gain_ref[...]).astype(bf16)
    out_ref[:, :feature] = grad_ref[...]
    vals = vals_ref[...]
    high = vals.astype(bf16).astype(f32)
    middle = (vals - high).astype(bf16).astype(f32)
    low = vals - high - middle
    rest = jnp.zeros((META - 4 * TOP, tokens), f32)
    meta = jnp.concatenate([ids_ref[...].astype(f32), high, middle, low, rest], axis=0)
    out_ref[:, feature:] = meta.T.astype(bf16)


def enter(resid, out_grad, gain, expert_ids, gate_vals):
    tokens, feature = resid.shape
    return pl.pallas_call(
        enter_kernel,
        out_shape=[
            jax.ShapeDtypeStruct((tokens, feature), bf16),
            jax.ShapeDtypeStruct((tokens, feature + META), bf16),
        ],
    )(resid, out_grad, gain.reshape(1, feature), expert_ids.T, gate_vals.T)


def pick_kernel(layout, first, offset, z_ref, *refs):
    pieces = sum(len(widths) for widths in layout)
    ins, (out_ref, target_ref, held, gates) = refs[:pieces], refs[-4:]
    rows, width = out_ref.shape[1:]
    half = width // 2
    tokens = ins[0].shape[0]

    @pl.when(pl.program_id(0) == 0)
    def _():
        own = lax.broadcasted_iota(jnp.int32, (PLANE, tokens), 0) * RING + z_ref[0]
        own = own.astype(f32)
        earlier = lax.broadcasted_iota(jnp.int32, (tokens, tokens), 0)
        earlier = earlier < lax.broadcasted_iota(jnp.int32, (tokens, tokens), 1)
        earlier = jnp.where(earlier, 1.0, 0.0).astype(bf16)
        at = 0
        for i, widths in enumerate(layout):
            lines = slice(i * tokens, (i + 1) * tokens)
            column = 0
            for piece in widths:
                ref = ins[at]
                data = piece
                if column + piece > width:
                    data = width - column
                    meta = ref[:, data:]
                held[lines, column : column + data] = ref[:, :data]
                column += data
                at += 1
            meta = meta.astype(f32).T
            value = meta[TOP : 2 * TOP] + meta[2 * TOP : 3 * TOP] + meta[3 * TOP : 4 * TOP]
            named = jnp.zeros((PLANE, tokens), f32)
            gate = jnp.zeros((PLANE, tokens), f32)
            for k in range(TOP):
                same = meta[k : k + 1] == own
                named = jnp.where(same, 1.0, named)
                gate = jnp.where(same, value[k : k + 1], gate)
            slot = jnp.dot(named.astype(bf16), earlier, preferred_element_type=f32)
            place = jnp.where(named > 0.5, slot + float((first + i) * CAPACITY), -1.0)
            target_ref[:, lines] = place
            gates[:, lines] = gate

    row_ids = (lax.broadcasted_iota(jnp.int32, (rows, held.shape[0]), 0) + offset).astype(f32)
    for i in range(out_ref.shape[0]):
        e = pl.program_id(0) * out_ref.shape[0] + i
        hit = row_ids == target_ref[pl.ds(e, 1), :]
        gate = jnp.sum(jnp.where(hit, gates[pl.ds(e, 1), :], 0.0), axis=1, keepdims=True)
        onehot = jnp.where(hit, 1.0, 0.0).astype(bf16)
        picked = jnp.dot(onehot, held[:, :half], preferred_element_type=f32)
        out_ref[i, :, :half] = picked.astype(bf16)
        picked = jnp.dot(onehot, held[:, half:], preferred_element_type=f32)
        out_ref[i, :, half:] = (picked * gate).astype(bf16)


def pick_rows(z, blocks, width, total, first=0, rows=None, into=None):
    count = len(blocks)
    tokens = blocks[0][0].shape[0]
    rows = rows or total
    at = total // rows - 1
    flat = [piece for block in blocks for piece in block]
    layout = tuple(tuple(piece.shape[1] for piece in block) for block in blocks)
    whole = [pl.BlockSpec(piece.shape, lambda e, z: (0, 0)) for piece in flat]
    return pl.pallas_call(
        functools.partial(pick_kernel, layout, first, total - rows),
        grid_spec=pltpu.PrefetchScalarGridSpec(
            num_scalar_prefetch=1,
            grid=(2,),
            in_specs=whole + [pl.BlockSpec(memory_space=pl.ANY)] * (into is not None),
            out_specs=[
                pl.BlockSpec((PLANE // 2, rows, width), lambda e, z: (e, at, 0)),
                pl.BlockSpec((PLANE, count * tokens), lambda e, z: (0, 0)),
            ],
            scratch_shapes=[
                pltpu.VMEM((count * tokens, width), bf16),
                pltpu.VMEM((PLANE, count * tokens), f32),
            ],
        ),
        out_shape=[
            jax.ShapeDtypeStruct((PLANE, total, width), bf16),
            jax.ShapeDtypeStruct((PLANE, count * tokens), f32),
        ],
        input_output_aliases={} if into is None else {1 + len(flat): 0},
        compiler_params=pltpu.CompilerParams(vmem_limit_bytes=56 << 20),
        cost_estimate=pl.CostEstimate(
            flops=2 * PLANE * rows * count * tokens * width,
            bytes_accessed=2 * width * (count * tokens + PLANE * rows),
            transcendentals=0,
        ),
    )(z.reshape(1), *flat, *([] if into is None else [into]))


def expert_kernel(got_ref, w_gate_ref, w_up_ref, w_down_ref, back_ref, slopes_ref, hidden_ref):
    feature = back_ref.shape[1]
    inner = hidden_ref.shape[1]
    rows_in, rows_grad = got_ref[:, :feature], got_ref[:, feature:]
    pre_gate = jnp.dot(rows_in, w_gate_ref[...], preferred_element_type=f32)
    pre_up = jnp.dot(rows_in, w_up_ref[...], preferred_element_type=f32)
    d_hidden = contract_last(rows_grad, w_down_ref[...])
    sigma = jax.nn.sigmoid(pre_gate)
    active = pre_gate * sigma
    hidden_ref[...] = (active * pre_up).astype(bf16)
    d_gate = (d_hidden * pre_up * (sigma * (1.0 + pre_gate * (1.0 - sigma)))).astype(bf16)
    d_up = (d_hidden * active).astype(bf16)
    for i in range(inner // 128):
        slopes_ref[:, 256 * i : 256 * i + 128] = d_gate[:, 128 * i : 128 * i + 128]
        slopes_ref[:, 256 * i + 128 : 256 * i + 256] = d_up[:, 128 * i : 128 * i + 128]
    back = contract_last(d_gate, w_gate_ref[...]) + contract_last(d_up, w_up_ref[...])
    back_ref[...] = back.astype(bf16)


def run_expert(got, w_gate, w_up, w_down, steps):
    total, width = got.shape
    feature, inner = w_gate.shape
    rows = total // steps
    return pl.pallas_call(
        expert_kernel,
        grid=(steps,),
        in_specs=[
            pl.BlockSpec((rows, width), lambda i: (i, 0)),
            pl.BlockSpec((feature, inner), lambda i: (0, 0)),
            pl.BlockSpec((feature, inner), lambda i: (0, 0)),
            pl.BlockSpec((inner, feature), lambda i: (0, 0)),
        ],
        out_specs=[
            pl.BlockSpec((rows, feature), lambda i: (i, 0)),
            pl.BlockSpec((rows, 2 * inner), lambda i: (i, 0)),
            pl.BlockSpec((rows, inner), lambda i: (i, 0)),
        ],
        out_shape=[
            jax.ShapeDtypeStruct((total, feature), bf16),
            jax.ShapeDtypeStruct((total, 2 * inner), bf16),
            jax.ShapeDtypeStruct((total, inner), bf16),
        ],
        compiler_params=pltpu.CompilerParams(vmem_limit_bytes=56 << 20),
        cost_estimate=pl.CostEstimate(
            flops=10 * total * feature * inner,
            bytes_accessed=2 * total * (width + feature + 3 * inner) + 6 * feature * inner,
            transcendentals=total * inner,
        ),
    )(got, w_gate, w_up, w_down)


def weights_kernel(core_ref, *refs):
    (x1, g1, s1, h1, x2, g2, s2, h2, other_ref, mine_ref) = refs
    feature = x1.shape[1]
    top = contract_rows(x1[...], s1[...]) + contract_rows(x2[...], s2[...])
    low = contract_rows(h1[...], g1[...]) + contract_rows(h2[...], g2[...])

    @pl.when(pl.program_id(0) < 2)
    def _():
        other_ref[0, :feature, :] = top.astype(bf16)
        other_ref[0, feature:, :] = low.astype(bf16)

    @pl.when(pl.program_id(0) >= 2)
    def _():
        mine_ref[0, :feature, :] = top
        mine_ref[0, feature:, :] = low


def weight_terms(ylo, core, near, far):
    specs, arrays, flops = [], [], 0
    for got, slopes, hidden in (near, far):
        rows, width = got.shape
        feature = width // 2
        inner = hidden.shape[1]
        share = feature // 4

        def block(s, core):
            return jnp.where(s % 2 == 0, 1 - core[1], core[1]) * 2 + jnp.where(s < 2, 1 - core[0], core[0])

        specs += [
            pl.BlockSpec((rows, feature), lambda s, core: (0, 0)),
            pl.BlockSpec((rows, share), lambda s, core: (0, 4 + block(s, core))),
            pl.BlockSpec((rows, share), lambda s, core: (0, block(s, core))),
            pl.BlockSpec((rows, inner), lambda s, core: (0, 0)),
        ]
        arrays += [got, got, slopes, hidden]
        flops += 2 * rows * feature * 3 * inner
    shape = (2, feature + inner, share)
    return pl.pallas_call(
        weights_kernel,
        grid_spec=pltpu.PrefetchScalarGridSpec(
            num_scalar_prefetch=1,
            grid=(4,),
            in_specs=specs,
            out_specs=[
                pl.BlockSpec((1,) + shape[1:], lambda s, core: (jnp.minimum(s, 1), 0, 0)),
                pl.BlockSpec((1,) + shape[1:], lambda s, core: (jnp.maximum(s - 2, 0), 0, 0)),
            ],
        ),
        out_shape=[jax.ShapeDtypeStruct(shape, bf16), jax.ShapeDtypeStruct(shape, f32)],
        compiler_params=pltpu.CompilerParams(vmem_limit_bytes=56 << 20),
        cost_estimate=pl.CostEstimate(flops=flops, bytes_accessed=16 << 20, transcendentals=0),
    )(jnp.stack([core, ylo]), *arrays)


def body(attn_out, resid, out_grad, gain, expert_ids, gate_vals, w_gate, w_up, w_down):
    tokens, feature = resid.shape
    z = lax.axis_index("z")
    core = lax.axis_index("core")
    ylo = lax.axis_index("ylo")
    yhi = lax.axis_index("yhi")
    w_gate, w_up, w_down = w_gate[0], w_up[0], w_down[0]

    own = enter(resid, out_grad, gain, expert_ids, gate_vals)
    right, left = [shift_z(a, 1) for a in own], [shift_z(a, -1) for a in own]
    gathered = {0: own, -1: right, 1: left}
    sent_near, target_near = pick_rows(z, [gathered[d] for d in NEAR], 2 * feature, 56)
    attn = attn_out.reshape(tokens, 2, 2, 4, 2, 64).transpose(1, 2, 4, 0, 3, 5).reshape(8, tokens, 256)
    attn = lax.all_to_all(attn, ("ylo", "core", "yhi"), split_axis=0, concat_axis=0, tiled=True)
    right, left = [shift_z(a, 1) for a in right], [shift_z(a, -1) for a in left]
    sent_near, attn, right, left = lax.optimization_barrier((sent_near, attn, right, left))
    gathered[-2], gathered[2] = right, left
    right, left = [shift_z(a, 1) for a in right], [shift_z(a, -1) for a in left]
    gathered[-3], gathered[3] = right, left
    sent_far, target_far = pick_rows(z, [gathered[d] for d in FAR[:-1]], 2 * feature, 96)
    sent_far, *last = lax.optimization_barrier((sent_far, shift_z(right[0], 1), shift_z(left[1], -1)))
    last = [gathered[3], last]
    sent_far, target_last = pick_rows(z, last, 2 * feature, 96, len(FAR) - 2, 32, sent_far)
    target_far = jnp.concatenate([target_far, target_last[:, tokens:]], axis=1)

    def over_plane(rows):
        return lax.all_to_all(rows, ("x", "yhi"), split_axis=0, concat_axis=0, tiled=True)

    got_near = over_plane(sent_near).reshape(-1, 2 * feature)
    got_near, sent_far = lax.optimization_barrier((got_near, sent_far))
    got_far = over_plane(sent_far).reshape(-1, 2 * feature)
    back_near, *saved_near = run_expert(got_near, w_gate, w_up, w_down, 2)
    back_near, got_far = lax.optimization_barrier((back_near, got_far))
    returned_near = over_plane(back_near.reshape(PLANE, -1, feature))
    back_far, *saved_far = run_expert(got_far, w_gate, w_up, w_down, 2)
    returned_near, back_far = lax.optimization_barrier((returned_near, back_far))
    returned_far = over_plane(back_far.reshape(PLANE, -1, feature))
    other, own = weight_terms(ylo, core, (got_near, *saved_near), (got_far, *saved_far))
    returned_far, other, own = lax.optimization_barrier((returned_far, other, own))

    terms = {}
    for target, deltas, returned in ((target_near, NEAR, returned_near), (target_far, FAR, returned_far)):
        rows = returned.shape[1]
        pick = (jnp.arange(rows, dtype=jnp.int32).astype(f32)[None, :, None] == target[:, None, :]).astype(bf16)
        term = contract_rows(pick.reshape(PLANE * rows, -1), returned.reshape(PLANE * rows, feature))
        for i, d in enumerate(deltas):
            terms[d] = term[i * tokens : (i + 1) * tokens]
    d_moe, other = ring_scatter(terms, other)
    from_core = swap(other, "core").astype(f32)
    beside = (own[0] + from_core[0]).astype(bf16)

    gain_f = gain[None, :]
    resid_f = resid.astype(f32)
    inv_rms = lax.rsqrt(jnp.mean(resid_f * resid_f, axis=1, keepdims=True) + epsilon)
    normed = resid_f * inv_rms
    d_norm = d_moe * gain_f
    inner = jnp.mean(d_norm * normed, axis=1, keepdims=True)
    d_resid = (out_grad.astype(f32) + inv_rms * (d_norm - normed * inner)).astype(bf16)

    attn = attn.reshape(2, 2, 2, tokens, 256)
    y = yhi * 2 + ylo
    pieces = []
    for step in (0, 1, 3, 2):
        block = d_resid if step == 0 else lax.ppermute(d_resid, ("ylo", "yhi"), y_peer(step))
        source = (y - step) % 4
        for crossed in (0, 1):
            piece = swap(block, "core") if crossed else block
            held = attn[source % 2, (core + crossed) % 2, source // 2]
            pieces.append((held, piece))
    part = contract_rows(
        jnp.concatenate([a for a, _ in pieces], axis=0), jnp.concatenate([b for _, b in pieces], axis=0)
    )
    part, beside = lax.optimization_barrier((part.astype(bf16), beside))
    total = own[1] + from_core[1] + swap(beside, "ylo").astype(f32)
    half = total.shape[1] // 2
    gate_out, up_out, down_out = total[None, :feature, :half], total[None, :feature, half:], total[None, feature:]
    part = part.reshape(32, 8, feature)
    part = lax.all_to_all(part, ("x", "z"), split_axis=0, concat_axis=0, tiled=True)
    projection_grad = jnp.sum(part.astype(f32), axis=0)
    return (d_resid, projection_grad, gate_out, up_out, down_out)


def solution(mesh):
    whole = Mesh(mesh.devices.reshape(2, 2, 4, 2, RING), AXES)
    tok = P(AXES, None)
    exp = ("x", "yhi", "z")
    weights = P(exp, None, None)
    in_specs = (tok, tok, tok, P(), tok, tok, weights, weights, weights)
    grads = P(exp, None, ("ylo", "core"))
    out_specs = (tok, tok, grads, grads, grads)
    return jax.shard_map(body, mesh=whole, in_specs=in_specs, out_specs=out_specs, check_vma=False)
```

```python
import functools

import jax
import jax.numpy as jnp
from jax import lax
from jax.experimental import pallas as pl
from jax.experimental.pallas import tpu as pltpu
from jax.sharding import Mesh, PartitionSpec as P

epsilon = 1e-06
AXES = ("ylo", "core", "x", "yhi", "z")
RING = 8
PLANE = 8
TOP = 8
CAPACITY = 18
META = 128
NEAR = (0, -1, 1)
FAR = (-2, 2, -3, 3, 4)
bf16 = jnp.bfloat16
f32 = jnp.float32


def contract_rows(left, right):
    return lax.dot_general(left, right, (((0,), (0,)), ((), ())), preferred_element_type=f32)


def contract_last(left, right):
    return lax.dot_general(left, right, (((1,), (1,)), ((), ())), preferred_element_type=f32)


def shift_z(block, step):
    return lax.ppermute(block, "z", [(i, (i + step) % RING) for i in range(RING)])


def swap(block, axis):
    return lax.ppermute(block, axis, [(0, 1), (1, 0)])


def y_peer(step):
    pairs = []
    for y in range(4):
        to = (y + step) % 4
        pairs.append(((y % 2) * 2 + y // 2, (to % 2) * 2 + to // 2))
    return pairs


def ring_scatter(blocks):
    half = blocks[4].shape[1] // 2
    far = blocks[4].astype(bf16)
    right, left = shift_z(blocks[3].astype(bf16), 1), shift_z(blocks[-3].astype(bf16), -1)
    far_right, far_left = shift_z(far[:, :half], 2).astype(f32), shift_z(far[:, half:], -2).astype(f32)
    right, left = blocks[2] + right.astype(f32), blocks[-2] + left.astype(f32)
    right = jnp.concatenate([right[:, :half] + far_right, right[:, half:]], axis=1)
    left = jnp.concatenate([left[:, :half], left[:, half:] + far_left], axis=1)
    right, left = shift_z(right.astype(bf16), 1), shift_z(left.astype(bf16), -1)
    right, left = blocks[1] + right.astype(f32), blocks[-1] + left.astype(f32)
    right, left = shift_z(right.astype(bf16), 1), shift_z(left.astype(bf16), -1)
    return blocks[0] + right.astype(f32) + left.astype(f32)


def enter_kernel(resid_ref, grad_ref, gain_ref, ids_ref, vals_ref, in_ref, out_ref):
    tokens, feature = resid_ref.shape
    resid = resid_ref[...].astype(f32)
    inv_rms = lax.rsqrt(jnp.mean(resid * resid, axis=1, keepdims=True) + epsilon)
    in_ref[...] = (resid * inv_rms * gain_ref[...]).astype(bf16)
    out_ref[:, :feature] = grad_ref[...]
    vals = vals_ref[...]
    high = vals.astype(bf16).astype(f32)
    middle = (vals - high).astype(bf16).astype(f32)
    low = vals - high - middle
    rest = jnp.zeros((META - 4 * TOP, tokens), f32)
    meta = jnp.concatenate([ids_ref[...].astype(f32), high, middle, low, rest], axis=0)
    out_ref[:, feature:] = meta.T.astype(bf16)


def enter(resid, out_grad, gain, expert_ids, gate_vals):
    tokens, feature = resid.shape
    return pl.pallas_call(
        enter_kernel,
        out_shape=[
            jax.ShapeDtypeStruct((tokens, feature), bf16),
            jax.ShapeDtypeStruct((tokens, feature + META), bf16),
        ],
    )(resid, out_grad, gain.reshape(1, feature), expert_ids.T, gate_vals.T)


def pick_kernel(layout, first, offset, z_ref, *refs):
    pieces = sum(len(widths) for widths in layout)
    ins, (out_ref, target_ref, held, gates) = refs[:pieces], refs[-4:]
    rows, width = out_ref.shape[1:]
    half = width // 2
    tokens = ins[0].shape[0]

    @pl.when(pl.program_id(0) == 0)
    def _():
        own = lax.broadcasted_iota(jnp.int32, (PLANE, tokens), 0) * RING + z_ref[0]
        own = own.astype(f32)
        earlier = lax.broadcasted_iota(jnp.int32, (tokens, tokens), 0)
        earlier = earlier < lax.broadcasted_iota(jnp.int32, (tokens, tokens), 1)
        earlier = jnp.where(earlier, 1.0, 0.0).astype(bf16)
        at = 0
        for i, widths in enumerate(layout):
            lines = slice(i * tokens, (i + 1) * tokens)
            column = 0
            for piece in widths:
                ref = ins[at]
                data = piece
                if column + piece > width:
                    data = width - column
                    meta = ref[:, data:]
                held[lines, column : column + data] = ref[:, :data]
                column += data
                at += 1
            meta = meta.astype(f32).T
            value = meta[TOP : 2 * TOP] + meta[2 * TOP : 3 * TOP] + meta[3 * TOP : 4 * TOP]
            named = jnp.zeros((PLANE, tokens), f32)
            gate = jnp.zeros((PLANE, tokens), f32)
            for k in range(TOP):
                same = meta[k : k + 1] == own
                named = jnp.where(same, 1.0, named)
                gate = jnp.where(same, value[k : k + 1], gate)
            slot = jnp.dot(named.astype(bf16), earlier, preferred_element_type=f32)
            place = jnp.where(named > 0.5, slot + float((first + i) * CAPACITY), -1.0)
            target_ref[:, lines] = place
            gates[:, lines] = gate

    row_ids = (lax.broadcasted_iota(jnp.int32, (rows, held.shape[0]), 0) + offset).astype(f32)
    for i in range(out_ref.shape[0]):
        e = pl.program_id(0) * out_ref.shape[0] + i
        hit = row_ids == target_ref[pl.ds(e, 1), :]
        gate = jnp.sum(jnp.where(hit, gates[pl.ds(e, 1), :], 0.0), axis=1, keepdims=True)
        onehot = jnp.where(hit, 1.0, 0.0).astype(bf16)
        picked = jnp.dot(onehot, held[:, :half], preferred_element_type=f32)
        out_ref[i, :, :half] = picked.astype(bf16)
        picked = jnp.dot(onehot, held[:, half:], preferred_element_type=f32)
        out_ref[i, :, half:] = (picked * gate).astype(bf16)


def pick_rows(z, blocks, width, total, first=0, rows=None, into=None):
    count = len(blocks)
    tokens = blocks[0][0].shape[0]
    rows = rows or total
    at = total // rows - 1
    flat = [piece for block in blocks for piece in block]
    layout = tuple(tuple(piece.shape[1] for piece in block) for block in blocks)
    whole = [pl.BlockSpec(piece.shape, lambda e, z: (0, 0)) for piece in flat]
    return pl.pallas_call(
        functools.partial(pick_kernel, layout, first, total - rows),
        grid_spec=pltpu.PrefetchScalarGridSpec(
            num_scalar_prefetch=1,
            grid=(2,),
            in_specs=whole + [pl.BlockSpec(memory_space=pl.ANY)] * (into is not None),
            out_specs=[
                pl.BlockSpec((PLANE // 2, rows, width), lambda e, z: (e, at, 0)),
                pl.BlockSpec((PLANE, count * tokens), lambda e, z: (0, 0)),
            ],
            scratch_shapes=[
                pltpu.VMEM((count * tokens, width), bf16),
                pltpu.VMEM((PLANE, count * tokens), f32),
            ],
        ),
        out_shape=[
            jax.ShapeDtypeStruct((PLANE, total, width), bf16),
            jax.ShapeDtypeStruct((PLANE, count * tokens), f32),
        ],
        input_output_aliases={} if into is None else {1 + len(flat): 0},
        compiler_params=pltpu.CompilerParams(vmem_limit_bytes=56 << 20),
        cost_estimate=pl.CostEstimate(
            flops=2 * PLANE * rows * count * tokens * width,
            bytes_accessed=2 * width * (count * tokens + PLANE * rows),
            transcendentals=0,
        ),
    )(z.reshape(1), *flat, *([] if into is None else [into]))


def expert_kernel(got_ref, w_gate_ref, w_up_ref, w_down_ref, back_ref, slopes_ref, hidden_ref):
    feature = back_ref.shape[1]
    inner = hidden_ref.shape[1]
    rows_in, rows_grad = got_ref[:, :feature], got_ref[:, feature:]
    pre_gate = jnp.dot(rows_in, w_gate_ref[...], preferred_element_type=f32)
    pre_up = jnp.dot(rows_in, w_up_ref[...], preferred_element_type=f32)
    d_hidden = contract_last(rows_grad, w_down_ref[...])
    sigma = jax.nn.sigmoid(pre_gate)
    active = pre_gate * sigma
    hidden_ref[...] = (active * pre_up).astype(bf16)
    d_gate = (d_hidden * pre_up * (sigma * (1.0 + pre_gate * (1.0 - sigma)))).astype(bf16)
    d_up = (d_hidden * active).astype(bf16)
    for i in range(inner // 128):
        slopes_ref[:, 256 * i : 256 * i + 128] = d_gate[:, 128 * i : 128 * i + 128]
        slopes_ref[:, 256 * i + 128 : 256 * i + 256] = d_up[:, 128 * i : 128 * i + 128]
    back = contract_last(d_gate, w_gate_ref[...]) + contract_last(d_up, w_up_ref[...])
    back_ref[...] = back.astype(bf16)


def run_expert(got, w_gate, w_up, w_down, steps):
    total, width = got.shape
    feature, inner = w_gate.shape
    rows = total // steps
    return pl.pallas_call(
        expert_kernel,
        grid=(steps,),
        in_specs=[
            pl.BlockSpec((rows, width), lambda i: (i, 0)),
            pl.BlockSpec((feature, inner), lambda i: (0, 0)),
            pl.BlockSpec((feature, inner), lambda i: (0, 0)),
            pl.BlockSpec((inner, feature), lambda i: (0, 0)),
        ],
        out_specs=[
            pl.BlockSpec((rows, feature), lambda i: (i, 0)),
            pl.BlockSpec((rows, 2 * inner), lambda i: (i, 0)),
            pl.BlockSpec((rows, inner), lambda i: (i, 0)),
        ],
        out_shape=[
            jax.ShapeDtypeStruct((total, feature), bf16),
            jax.ShapeDtypeStruct((total, 2 * inner), bf16),
            jax.ShapeDtypeStruct((total, inner), bf16),
        ],
        compiler_params=pltpu.CompilerParams(vmem_limit_bytes=56 << 20),
        cost_estimate=pl.CostEstimate(
            flops=10 * total * feature * inner,
            bytes_accessed=2 * total * (width + feature + 3 * inner) + 6 * feature * inner,
            transcendentals=total * inner,
        ),
    )(got, w_gate, w_up, w_down)


def weights_kernel(core_ref, *refs):
    (x1, g1, s1, h1, x2, g2, s2, h2, other_ref, mine_ref) = refs
    feature = x1.shape[1]
    top = contract_rows(x1[...], s1[...]) + contract_rows(x2[...], s2[...])
    low = contract_rows(h1[...], g1[...]) + contract_rows(h2[...], g2[...])

    @pl.when(pl.program_id(0) < 2)
    def _():
        other_ref[0, :feature, :] = top.astype(bf16)
        other_ref[0, feature:, :] = low.astype(bf16)

    @pl.when(pl.program_id(0) >= 2)
    def _():
        mine_ref[0, :feature, :] = top
        mine_ref[0, feature:, :] = low


def weight_terms(ylo, core, near, far):
    specs, arrays, flops = [], [], 0
    for got, slopes, hidden in (near, far):
        rows, width = got.shape
        feature = width // 2
        inner = hidden.shape[1]
        share = feature // 4

        def block(s, core):
            return jnp.where(s % 2 == 0, 1 - core[1], core[1]) * 2 + jnp.where(s < 2, 1 - core[0], core[0])

        specs += [
            pl.BlockSpec((rows, feature), lambda s, core: (0, 0)),
            pl.BlockSpec((rows, share), lambda s, core: (0, 4 + block(s, core))),
            pl.BlockSpec((rows, share), lambda s, core: (0, block(s, core))),
            pl.BlockSpec((rows, inner), lambda s, core: (0, 0)),
        ]
        arrays += [got, got, slopes, hidden]
        flops += 2 * rows * feature * 3 * inner
    shape = (2, feature + inner, share)
    return pl.pallas_call(
        weights_kernel,
        grid_spec=pltpu.PrefetchScalarGridSpec(
            num_scalar_prefetch=1,
            grid=(4,),
            in_specs=specs,
            out_specs=[
                pl.BlockSpec((1,) + shape[1:], lambda s, core: (jnp.minimum(s, 1), 0, 0)),
                pl.BlockSpec((1,) + shape[1:], lambda s, core: (jnp.maximum(s - 2, 0), 0, 0)),
            ],
        ),
        out_shape=[jax.ShapeDtypeStruct(shape, bf16), jax.ShapeDtypeStruct(shape, f32)],
        compiler_params=pltpu.CompilerParams(vmem_limit_bytes=56 << 20),
        cost_estimate=pl.CostEstimate(flops=flops, bytes_accessed=16 << 20, transcendentals=0),
    )(jnp.stack([core, ylo]), *arrays)


def body(attn_out, resid, out_grad, gain, expert_ids, gate_vals, w_gate, w_up, w_down):
    tokens, feature = resid.shape
    z = lax.axis_index("z")
    core = lax.axis_index("core")
    ylo = lax.axis_index("ylo")
    yhi = lax.axis_index("yhi")
    w_gate, w_up, w_down = w_gate[0], w_up[0], w_down[0]

    own = enter(resid, out_grad, gain, expert_ids, gate_vals)
    right, left = [shift_z(a, 1) for a in own], [shift_z(a, -1) for a in own]
    gathered = {0: own, -1: right, 1: left}
    sent_near, target_near = pick_rows(z, [gathered[d] for d in NEAR], 2 * feature, 56)
    attn = attn_out.reshape(tokens, 2, 2, 4, 2, 64).transpose(1, 2, 4, 0, 3, 5).reshape(8, tokens, 256)
    attn = lax.all_to_all(attn, ("ylo", "core", "yhi"), split_axis=0, concat_axis=0, tiled=True)
    right, left = [shift_z(a, 1) for a in right], [shift_z(a, -1) for a in left]
    sent_near, attn, right, left = lax.optimization_barrier((sent_near, attn, right, left))
    gathered[-2], gathered[2] = right, left
    right, left = [shift_z(a, 1) for a in right], [shift_z(a, -1) for a in left]
    gathered[-3], gathered[3] = right, left
    sent_far, target_far = pick_rows(z, [gathered[d] for d in FAR[:-1]], 2 * feature, 96)
    sent_far, *last = lax.optimization_barrier((sent_far, shift_z(right[0], 1), shift_z(left[1], -1)))
    last = [gathered[3], last]
    sent_far, target_last = pick_rows(z, last, 2 * feature, 96, len(FAR) - 2, 32, sent_far)
    target_far = jnp.concatenate([target_far, target_last[:, tokens:]], axis=1)

    def over_plane(rows):
        return lax.all_to_all(rows, ("x", "yhi"), split_axis=0, concat_axis=0, tiled=True)

    got_near = over_plane(sent_near).reshape(-1, 2 * feature)
    got_near, sent_far = lax.optimization_barrier((got_near, sent_far))
    got_far = over_plane(sent_far).reshape(-1, 2 * feature)
    back_near, *saved_near = run_expert(got_near, w_gate, w_up, w_down, 2)
    back_near, got_far = lax.optimization_barrier((back_near, got_far))
    returned_near = over_plane(back_near.reshape(PLANE, -1, feature))
    back_far, *saved_far = run_expert(got_far, w_gate, w_up, w_down, 2)
    returned_near, back_far = lax.optimization_barrier((returned_near, back_far))
    returned_far = over_plane(back_far.reshape(PLANE, -1, feature))
    other, own = weight_terms(ylo, core, (got_near, *saved_near), (got_far, *saved_far))
    returned_far, other, own = lax.optimization_barrier((returned_far, other, own))

    from_core = swap(other, "core").astype(f32)
    beside = (own[0] + from_core[0]).astype(bf16)

    terms = {}
    for target, deltas, returned in ((target_near, NEAR, returned_near), (target_far, FAR, returned_far)):
        rows = returned.shape[1]
        pick = (jnp.arange(rows, dtype=jnp.int32).astype(f32)[None, :, None] == target[:, None, :]).astype(bf16)
        term = contract_rows(pick.reshape(PLANE * rows, -1), returned.reshape(PLANE * rows, feature))
        for i, d in enumerate(deltas):
            terms[d] = term[i * tokens : (i + 1) * tokens]
    d_moe = ring_scatter(terms)
    gain_f = gain[None, :]
    resid_f = resid.astype(f32)
    inv_rms = lax.rsqrt(jnp.mean(resid_f * resid_f, axis=1, keepdims=True) + epsilon)
    normed = resid_f * inv_rms
    d_norm = d_moe * gain_f
    inner = jnp.mean(d_norm * normed, axis=1, keepdims=True)
    d_resid = (out_grad.astype(f32) + inv_rms * (d_norm - normed * inner)).astype(bf16)

    attn = attn.reshape(2, 2, 2, tokens, 256)
    y = yhi * 2 + ylo
    pieces = []
    for step in (0, 1, 3, 2):
        block = d_resid if step == 0 else lax.ppermute(d_resid, ("ylo", "yhi"), y_peer(step))
        source = (y - step) % 4
        for crossed in (0, 1):
            piece = swap(block, "core") if crossed else block
            held = attn[source % 2, (core + crossed) % 2, source // 2]
            pieces.append((held, piece))
    part = contract_rows(
        jnp.concatenate([a for a, _ in pieces], axis=0), jnp.concatenate([b for _, b in pieces], axis=0)
    )
    part, beside = lax.optimization_barrier((part.astype(bf16), beside))
    total = own[1] + from_core[1] + swap(beside, "ylo").astype(f32)
    half = total.shape[1] // 2
    gate_out, up_out, down_out = total[None, :feature, :half], total[None, :feature, half:], total[None, feature:]
    part = part.reshape(32, 8, feature)
    part = lax.all_to_all(part, ("x", "z"), split_axis=0, concat_axis=0, tiled=True)
    projection_grad = jnp.sum(part.astype(f32), axis=0)
    return (d_resid, projection_grad, gate_out, up_out, down_out)


def solution(mesh):
    whole = Mesh(mesh.devices.reshape(2, 2, 4, 2, RING), AXES)
    tok = P(AXES, None)
    exp = ("x", "yhi", "z")
    weights = P(exp, None, None)
    in_specs = (tok, tok, tok, P(), tok, tok, weights, weights, weights)
    grads = P(exp, None, ("ylo", "core"))
    out_specs = (tok, tok, grads, grads, grads)
    return jax.shard_map(body, mesh=whole, in_specs=in_specs, out_specs=out_specs, check_vma=False)
```

```python
import functools

import jax
import jax.numpy as jnp
from jax import lax
from jax.experimental import pallas as pl
from jax.experimental.pallas import tpu as pltpu
from jax.sharding import Mesh, PartitionSpec as P

epsilon = 1e-06
AXES = ("ylo", "core", "x", "yhi", "z")
RING = 8
PLANE = 8
TOP = 8
CAPACITY = 18
META = 128
NEAR = (0, -1, 1)
FAR = (-2, 2, -3, 3, 4)
bf16 = jnp.bfloat16
f32 = jnp.float32


def contract_rows(left, right):
    return lax.dot_general(left, right, (((0,), (0,)), ((), ())), preferred_element_type=f32)


def contract_last(left, right):
    return lax.dot_general(left, right, (((1,), (1,)), ((), ())), preferred_element_type=f32)


def shift_z(block, step):
    return lax.ppermute(block, "z", [(i, (i + step) % RING) for i in range(RING)])


def swap(block, axis):
    return lax.ppermute(block, axis, [(0, 1), (1, 0)])


def y_peer(step):
    pairs = []
    for y in range(4):
        to = (y + step) % 4
        pairs.append(((y % 2) * 2 + y // 2, (to % 2) * 2 + to // 2))
    return pairs


def ring_scatter(blocks):
    half = blocks[4].shape[1] // 2
    far = blocks[4].astype(bf16)
    right, left = shift_z(blocks[3].astype(bf16), 1), shift_z(blocks[-3].astype(bf16), -1)
    far_right, far_left = shift_z(far[:, :half], 2).astype(f32), shift_z(far[:, half:], -2).astype(f32)
    right, left = blocks[2] + right.astype(f32), blocks[-2] + left.astype(f32)
    right = jnp.concatenate([right[:, :half] + far_right, right[:, half:]], axis=1)
    left = jnp.concatenate([left[:, :half], left[:, half:] + far_left], axis=1)
    right, left = shift_z(right.astype(bf16), 1), shift_z(left.astype(bf16), -1)
    right, left = blocks[1] + right.astype(f32), blocks[-1] + left.astype(f32)
    right, left = shift_z(right.astype(bf16), 1), shift_z(left.astype(bf16), -1)
    return blocks[0] + right.astype(f32) + left.astype(f32)


def enter_kernel(resid_ref, grad_ref, gain_ref, ids_ref, vals_ref, in_ref, out_ref):
    tokens, feature = resid_ref.shape
    resid = resid_ref[...].astype(f32)
    inv_rms = lax.rsqrt(jnp.mean(resid * resid, axis=1, keepdims=True) + epsilon)
    in_ref[...] = (resid * inv_rms * gain_ref[...]).astype(bf16)
    out_ref[:, :feature] = grad_ref[...]
    vals = vals_ref[...]
    high = vals.astype(bf16).astype(f32)
    middle = (vals - high).astype(bf16).astype(f32)
    low = vals - high - middle
    rest = jnp.zeros((META - 4 * TOP, tokens), f32)
    meta = jnp.concatenate([ids_ref[...].astype(f32), high, middle, low, rest], axis=0)
    out_ref[:, feature:] = meta.T.astype(bf16)


def enter(resid, out_grad, gain, expert_ids, gate_vals):
    tokens, feature = resid.shape
    return pl.pallas_call(
        enter_kernel,
        out_shape=[
            jax.ShapeDtypeStruct((tokens, feature), bf16),
            jax.ShapeDtypeStruct((tokens, feature + META), bf16),
        ],
    )(resid, out_grad, gain.reshape(1, feature), expert_ids.T, gate_vals.T)


def pick_kernel(layout, first, offset, z_ref, *refs):
    pieces = sum(len(widths) for widths in layout)
    ins, (out_ref, target_ref, held, gates) = refs[:pieces], refs[-4:]
    rows, width = out_ref.shape[1:]
    half = width // 2
    tokens = ins[0].shape[0]

    @pl.when(pl.program_id(0) == 0)
    def _():
        own = lax.broadcasted_iota(jnp.int32, (PLANE, tokens), 0) * RING + z_ref[0]
        own = own.astype(f32)
        earlier = lax.broadcasted_iota(jnp.int32, (tokens, tokens), 0)
        earlier = earlier < lax.broadcasted_iota(jnp.int32, (tokens, tokens), 1)
        earlier = jnp.where(earlier, 1.0, 0.0).astype(bf16)
        at = 0
        for i, widths in enumerate(layout):
            lines = slice(i * tokens, (i + 1) * tokens)
            column = 0
            for piece in widths:
                ref = ins[at]
                data = piece
                if column + piece > width:
                    data = width - column
                    meta = ref[:, data:]
                held[lines, column : column + data] = ref[:, :data]
                column += data
                at += 1
            meta = meta.astype(f32).T
            value = meta[TOP : 2 * TOP] + meta[2 * TOP : 3 * TOP] + meta[3 * TOP : 4 * TOP]
            named = jnp.zeros((PLANE, tokens), f32)
            gate = jnp.zeros((PLANE, tokens), f32)
            for k in range(TOP):
                same = meta[k : k + 1] == own
                named = jnp.where(same, 1.0, named)
                gate = jnp.where(same, value[k : k + 1], gate)
            slot = jnp.dot(named.astype(bf16), earlier, preferred_element_type=f32)
            place = jnp.where(named > 0.5, slot + float((first + i) * CAPACITY), -1.0)
            target_ref[:, lines] = place
            gates[:, lines] = gate

    row_ids = (lax.broadcasted_iota(jnp.int32, (rows, held.shape[0]), 0) + offset).astype(f32)
    each = out_ref.shape[0]
    start = pl.program_id(0) * each

    @pl.loop(0, each)
    def _(i):
        e = start + i
        hit = row_ids == target_ref[pl.ds(e, 1), :]
        gate = jnp.sum(jnp.where(hit, gates[pl.ds(e, 1), :], 0.0), axis=1, keepdims=True)
        onehot = jnp.where(hit, 1.0, 0.0).astype(bf16)
        picked = jnp.dot(onehot, held[:, :half], preferred_element_type=f32)
        out_ref[i, :, :half] = picked.astype(bf16)
        picked = jnp.dot(onehot, held[:, half:], preferred_element_type=f32)
        out_ref[i, :, half:] = (picked * gate).astype(bf16)


def pick_rows(z, blocks, width, total, first=0, rows=None, into=None):
    count = len(blocks)
    tokens = blocks[0][0].shape[0]
    rows = rows or total
    at = total // rows - 1
    flat = [piece for block in blocks for piece in block]
    layout = tuple(tuple(piece.shape[1] for piece in block) for block in blocks)
    whole = [pl.BlockSpec(piece.shape, lambda e, z: (0, 0)) for piece in flat]
    return pl.pallas_call(
        functools.partial(pick_kernel, layout, first, total - rows),
        grid_spec=pltpu.PrefetchScalarGridSpec(
            num_scalar_prefetch=1,
            grid=(2,),
            in_specs=whole + [pl.BlockSpec(memory_space=pl.ANY)] * (into is not None),
            out_specs=[
                pl.BlockSpec((PLANE // 2, rows, width), lambda e, z: (e, at, 0)),
                pl.BlockSpec((PLANE, count * tokens), lambda e, z: (0, 0)),
            ],
            scratch_shapes=[
                pltpu.VMEM((count * tokens, width), bf16),
                pltpu.VMEM((PLANE, count * tokens), f32),
            ],
        ),
        out_shape=[
            jax.ShapeDtypeStruct((PLANE, total, width), bf16),
            jax.ShapeDtypeStruct((PLANE, count * tokens), f32),
        ],
        input_output_aliases={} if into is None else {1 + len(flat): 0},
        compiler_params=pltpu.CompilerParams(vmem_limit_bytes=56 << 20),
        cost_estimate=pl.CostEstimate(
            flops=2 * PLANE * rows * count * tokens * width,
            bytes_accessed=2 * width * (count * tokens + PLANE * rows),
            transcendentals=0,
        ),
    )(z.reshape(1), *flat, *([] if into is None else [into]))


def expert_kernel(got_ref, w_gate_ref, w_up_ref, w_down_ref, back_ref, slopes_ref, hidden_ref):
    feature = back_ref.shape[1]
    inner = hidden_ref.shape[1]
    rows_in, rows_grad = got_ref[:, :feature], got_ref[:, feature:]
    pre_gate = jnp.dot(rows_in, w_gate_ref[...], preferred_element_type=f32)
    pre_up = jnp.dot(rows_in, w_up_ref[...], preferred_element_type=f32)
    d_hidden = contract_last(rows_grad, w_down_ref[...])
    sigma = jax.nn.sigmoid(pre_gate)
    active = pre_gate * sigma
    hidden_ref[...] = (active * pre_up).astype(bf16)
    d_gate = (d_hidden * pre_up * (sigma * (1.0 + pre_gate * (1.0 - sigma)))).astype(bf16)
    d_up = (d_hidden * active).astype(bf16)
    for i in range(inner // 128):
        slopes_ref[:, 256 * i : 256 * i + 128] = d_gate[:, 128 * i : 128 * i + 128]
        slopes_ref[:, 256 * i + 128 : 256 * i + 256] = d_up[:, 128 * i : 128 * i + 128]
    back = contract_last(d_gate, w_gate_ref[...]) + contract_last(d_up, w_up_ref[...])
    back_ref[...] = back.astype(bf16)


def run_expert(got, w_gate, w_up, w_down, steps):
    total, width = got.shape
    feature, inner = w_gate.shape
    rows = total // steps
    return pl.pallas_call(
        expert_kernel,
        grid=(steps,),
        in_specs=[
            pl.BlockSpec((rows, width), lambda i: (i, 0)),
            pl.BlockSpec((feature, inner), lambda i: (0, 0)),
            pl.BlockSpec((feature, inner), lambda i: (0, 0)),
            pl.BlockSpec((inner, feature), lambda i: (0, 0)),
        ],
        out_specs=[
            pl.BlockSpec((rows, feature), lambda i: (i, 0)),
            pl.BlockSpec((rows, 2 * inner), lambda i: (i, 0)),
            pl.BlockSpec((rows, inner), lambda i: (i, 0)),
        ],
        out_shape=[
            jax.ShapeDtypeStruct((total, feature), bf16),
            jax.ShapeDtypeStruct((total, 2 * inner), bf16),
            jax.ShapeDtypeStruct((total, inner), bf16),
        ],
        compiler_params=pltpu.CompilerParams(vmem_limit_bytes=56 << 20),
        cost_estimate=pl.CostEstimate(
            flops=10 * total * feature * inner,
            bytes_accessed=2 * total * (width + feature + 3 * inner) + 6 * feature * inner,
            transcendentals=total * inner,
        ),
    )(got, w_gate, w_up, w_down)


def weights_kernel(core_ref, *refs):
    (x1, g1, s1, h1, x2, g2, s2, h2, other_ref, mine_ref) = refs
    feature = x1.shape[1]
    top = contract_rows(x1[...], s1[...]) + contract_rows(x2[...], s2[...])
    low = contract_rows(h1[...], g1[...]) + contract_rows(h2[...], g2[...])

    @pl.when(pl.program_id(0) < 2)
    def _():
        other_ref[0, :feature, :] = top.astype(bf16)
        other_ref[0, feature:, :] = low.astype(bf16)

    @pl.when(pl.program_id(0) >= 2)
    def _():
        mine_ref[0, :feature, :] = top
        mine_ref[0, feature:, :] = low


def weight_terms(ylo, core, near, far):
    specs, arrays, flops = [], [], 0
    for got, slopes, hidden in (near, far):
        rows, width = got.shape
        feature = width // 2
        inner = hidden.shape[1]
        share = feature // 4

        def block(s, core):
            return jnp.where(s % 2 == 0, 1 - core[1], core[1]) * 2 + jnp.where(s < 2, 1 - core[0], core[0])

        specs += [
            pl.BlockSpec((rows, feature), lambda s, core: (0, 0)),
            pl.BlockSpec((rows, share), lambda s, core: (0, 4 + block(s, core))),
            pl.BlockSpec((rows, share), lambda s, core: (0, block(s, core))),
            pl.BlockSpec((rows, inner), lambda s, core: (0, 0)),
        ]
        arrays += [got, got, slopes, hidden]
        flops += 2 * rows * feature * 3 * inner
    shape = (2, feature + inner, share)
    return pl.pallas_call(
        weights_kernel,
        grid_spec=pltpu.PrefetchScalarGridSpec(
            num_scalar_prefetch=1,
            grid=(4,),
            in_specs=specs,
            out_specs=[
                pl.BlockSpec((1,) + shape[1:], lambda s, core: (jnp.minimum(s, 1), 0, 0)),
                pl.BlockSpec((1,) + shape[1:], lambda s, core: (jnp.maximum(s - 2, 0), 0, 0)),
            ],
        ),
        out_shape=[jax.ShapeDtypeStruct(shape, bf16), jax.ShapeDtypeStruct(shape, f32)],
        compiler_params=pltpu.CompilerParams(vmem_limit_bytes=56 << 20),
        cost_estimate=pl.CostEstimate(flops=flops, bytes_accessed=16 << 20, transcendentals=0),
    )(jnp.stack([core, ylo]), *arrays)


def body(attn_out, resid, out_grad, gain, expert_ids, gate_vals, w_gate, w_up, w_down):
    tokens, feature = resid.shape
    z = lax.axis_index("z")
    core = lax.axis_index("core")
    ylo = lax.axis_index("ylo")
    yhi = lax.axis_index("yhi")
    w_gate, w_up, w_down = w_gate[0], w_up[0], w_down[0]

    own = enter(resid, out_grad, gain, expert_ids, gate_vals)
    right, left = [shift_z(a, 1) for a in own], [shift_z(a, -1) for a in own]
    gathered = {0: own, -1: right, 1: left}
    sent_near, target_near = pick_rows(z, [gathered[d] for d in NEAR], 2 * feature, 56)
    attn = attn_out.reshape(tokens, 2, 2, 4, 2, 64).transpose(1, 2, 4, 0, 3, 5).reshape(8, tokens, 256)
    attn = lax.all_to_all(attn, ("ylo", "core", "yhi"), split_axis=0, concat_axis=0, tiled=True)
    right, left = [shift_z(a, 1) for a in right], [shift_z(a, -1) for a in left]
    sent_near, attn, right, left = lax.optimization_barrier((sent_near, attn, right, left))
    gathered[-2], gathered[2] = right, left
    right, left = [shift_z(a, 1) for a in right], [shift_z(a, -1) for a in left]
    gathered[-3], gathered[3] = right, left
    sent_far, target_far = pick_rows(z, [gathered[d] for d in FAR[:-1]], 2 * feature, 96)
    sent_far, *last = lax.optimization_barrier((sent_far, shift_z(right[0], 1), shift_z(left[1], -1)))
    last = [gathered[3], last]
    sent_far, target_last = pick_rows(z, last, 2 * feature, 96, len(FAR) - 2, 32, sent_far)
    target_far = jnp.concatenate([target_far, target_last[:, tokens:]], axis=1)

    def over_plane(rows):
        return lax.all_to_all(rows, ("x", "yhi"), split_axis=0, concat_axis=0, tiled=True)

    got_near = over_plane(sent_near).reshape(-1, 2 * feature)
    got_near, sent_far = lax.optimization_barrier((got_near, sent_far))
    got_far = over_plane(sent_far).reshape(-1, 2 * feature)
    back_near, *saved_near = run_expert(got_near, w_gate, w_up, w_down, 2)
    back_near, got_far = lax.optimization_barrier((back_near, got_far))
    returned_near = over_plane(back_near.reshape(PLANE, -1, feature))
    back_far, *saved_far = run_expert(got_far, w_gate, w_up, w_down, 2)
    returned_near, back_far = lax.optimization_barrier((returned_near, back_far))
    returned_far = over_plane(back_far.reshape(PLANE, -1, feature))
    other, own = weight_terms(ylo, core, (got_near, *saved_near), (got_far, *saved_far))
    returned_far, other, own = lax.optimization_barrier((returned_far, other, own))

    from_core = swap(other, "core").astype(f32)
    beside = (own[0] + from_core[0]).astype(bf16)

    terms = {}
    for target, deltas, returned in ((target_near, NEAR, returned_near), (target_far, FAR, returned_far)):
        rows = returned.shape[1]
        pick = (jnp.arange(rows, dtype=jnp.int32).astype(f32)[None, :, None] == target[:, None, :]).astype(bf16)
        term = contract_rows(pick.reshape(PLANE * rows, -1), returned.reshape(PLANE * rows, feature))
        for i, d in enumerate(deltas):
            terms[d] = term[i * tokens : (i + 1) * tokens]
    d_moe = ring_scatter(terms)
    gain_f = gain[None, :]
    resid_f = resid.astype(f32)
    inv_rms = lax.rsqrt(jnp.mean(resid_f * resid_f, axis=1, keepdims=True) + epsilon)
    normed = resid_f * inv_rms
    d_norm = d_moe * gain_f
    inner = jnp.mean(d_norm * normed, axis=1, keepdims=True)
    d_resid = (out_grad.astype(f32) + inv_rms * (d_norm - normed * inner)).astype(bf16)

    attn = attn.reshape(2, 2, 2, tokens, 256)
    y = yhi * 2 + ylo
    pieces = []
    for step in (0, 1, 3, 2):
        block = d_resid if step == 0 else lax.ppermute(d_resid, ("ylo", "yhi"), y_peer(step))
        source = (y - step) % 4
        for crossed in (0, 1):
            piece = swap(block, "core") if crossed else block
            held = attn[source % 2, (core + crossed) % 2, source // 2]
            pieces.append((held, piece))
    part = contract_rows(
        jnp.concatenate([a for a, _ in pieces], axis=0), jnp.concatenate([b for _, b in pieces], axis=0)
    )
    part, beside = lax.optimization_barrier((part.astype(bf16), beside))
    total = own[1] + from_core[1] + swap(beside, "ylo").astype(f32)
    half = total.shape[1] // 2
    gate_out, up_out, down_out = total[None, :feature, :half], total[None, :feature, half:], total[None, feature:]
    part = part.reshape(32, 8, feature)
    part = lax.all_to_all(part, ("x", "z"), split_axis=0, concat_axis=0, tiled=True)
    projection_grad = jnp.sum(part.astype(f32), axis=0)
    return (d_resid, projection_grad, gate_out, up_out, down_out)


def solution(mesh):
    whole = Mesh(mesh.devices.reshape(2, 2, 4, 2, RING), AXES)
    tok = P(AXES, None)
    exp = ("x", "yhi", "z")
    weights = P(exp, None, None)
    in_specs = (tok, tok, tok, P(), tok, tok, weights, weights, weights)
    grads = P(exp, None, ("ylo", "core"))
    out_specs = (tok, tok, grads, grads, grads)
    return jax.shard_map(body, mesh=whole, in_specs=in_specs, out_specs=out_specs, check_vma=False)
```
